256 devices in a mesh: blk: 32 (over y, z), head: 8 (over x, core).
Axes of the slice: x: 4, y: 4, z: 8, core: 2. Of those that a mesh axis runs over, the one named last changes fastest.
Arguments:
- queries: bfloat16 [24576, 64, 128], P(('blk', 'head')), may hold values from -6 to 6
- keys: bfloat16 [24576, 8, 128], P(('blk', 'head')), may hold values from -6 to 6
- values: bfloat16 [24576, 8, 128], P(('blk', 'head')), may hold values from -6 to 6
- out_grad: bfloat16 [24576, 64, 128], P(('blk', 'head')), may hold values from -6 to 6
- rand_blocks: int32 [192, 8, 3], replicated, may hold values from 0 to 191, as said below
- global_blocks: int32 [2], replicated, may hold values from 0 to 191
Outputs:
- attn_out: bfloat16 [24576, 64, 128], P(('blk', 'head'))
- query_grad: bfloat16 [24576, 64, 128], P(('blk', 'head'))
- key_grad: bfloat16 [24576, 8, 128], P(('blk', 'head'))
- value_grad: bfloat16 [24576, 8, 128], P(('blk', 'head'))
The draws below stay inside these ranges and needn't reach their ends.
Inputs may be any that keep to these rules, and one draw needn't show every extreme that they name: `rand_blocks`: for every shard of 6 query blocks and every KV head, the 18 random entries name blocks of any one shard at most 1 times, and some shard exactly 1 times.
All inputs are finite; a program needn't handle non-finite values.
Results may differ from the reference program's by a relative error of at most 0.02.
Values may be sent and summed in bfloat16 or wider, within the bound.
A program may use at most 128 MiB of HBM per device.

```python
import math
import jax
import jax.numpy as jnp
from jax import lax

HQ = 64
KVH = 8
DH = 128
BS = 128
RAND = 3
QB = 6
NB = 192
SEQ = 24576
GROUP = 8


def draw_keys(key, part):
    row_scale = jnp.exp(jax.random.uniform(jax.random.fold_in(key, 7), (SEQ, 1, 1), minval=math.log(0.3), maxval=math.log(3.0)))
    result = jax.random.truncated_normal(jax.random.fold_in(key, 8), -2.0, 2.0, (SEQ, KVH, DH)) * row_scale
    return result.astype(jnp.bfloat16)


def draw_queries(key, part):
    result = jax.random.truncated_normal(jax.random.fold_in(key, 9), -4.0, 4.0, (SEQ, HQ, DH))
    return result.astype(jnp.bfloat16)


def draw_rand_blocks(key, part):
    shard_count = NB // QB
    count = QB * RAND
    key_grid = jax.random.split(jax.random.fold_in(key, 3), shard_count * KVH)
    orders = jax.vmap(lambda single: jax.random.permutation(single, count))(key_grid)
    offsets = jax.random.randint(jax.random.fold_in(key, 4), (shard_count * KVH, 1), 0, shard_count)
    owners = (orders + offsets) % shard_count
    within = jax.random.randint(jax.random.fold_in(key, 5), (shard_count * KVH, count), 0, QB)
    blocks = (owners * QB + within).reshape(shard_count, KVH, QB, RAND).transpose(0, 2, 1, 3)
    return blocks.reshape(NB, KVH, RAND).astype(jnp.int32)


def shard_levels(key, dims, cuts, low, high):
    gain, own = 1.0, jax.random.fold_in(key, 6)
    for dim, shards_of in cuts:
        heights = jnp.exp(jax.random.uniform(jax.random.fold_in(own, dim), (shards_of,), jnp.float32, low / len(cuts), high / len(cuts)))
        gain = gain * jnp.repeat(heights, dims[dim] // shards_of).reshape([-1 if axis == dim else 1 for axis in range(len(dims))])
    return gain


def gaussian(stream_key, dims, width, most, shards=(), kind=jnp.bfloat16):
    level = shard_levels(stream_key, dims, shards, -0.22, 0.18) if shards else 1.0
    values = jax.random.normal(stream_key, dims, jnp.float32) * width * level
    return jnp.minimum(jnp.maximum(values, -most), most).astype(kind)


def setup_inputs(seed: int = 0) -> dict:
    key_list = jax.random.split(jax.random.key(seed), 7)
    queries = draw_queries(jax.random.fold_in(key_list[6], 71), 0)
    keys = draw_keys(jax.random.fold_in(key_list[6], 71), 0)
    values = gaussian(key_list[2], (SEQ, KVH, DH), 1.0, 6.0, ((0, 256),))
    out_grad = gaussian(key_list[3], (SEQ, HQ, DH), 1.0, 6.0, ((0, 256),))
    rand_blocks = draw_rand_blocks(jax.random.fold_in(key_list[6], 71), 0)
    global_blocks = jax.random.randint(key_list[5], (2,), 0, NB).astype(jnp.int32)
    return {"queries": queries, "keys": keys, "values": values, "out_grad": out_grad, "rand_blocks": rand_blocks, "global_blocks": global_blocks}


def attend_rows(query_blk, key_blk, value_blk, grad_blk, scaling):
    query_f = query_blk.astype(jnp.float32)
    key_f = key_blk.astype(jnp.float32)
    value_f = value_blk.astype(jnp.float32)
    grad_f = grad_blk.astype(jnp.float32)
    scores = jnp.einsum('tgad,gkd->gatk', query_f, key_f) * scaling
    peak = lax.optimization_barrier(jnp.max(scores, axis=-1, keepdims=True))
    expo = jnp.exp(scores - peak)
    probs = expo / lax.optimization_barrier(jnp.sum(expo, axis=-1, keepdims=True))
    probs_b = lax.optimization_barrier(probs.astype(jnp.bfloat16)).astype(jnp.float32)
    output = lax.optimization_barrier(jnp.einsum('gatk,gkd->tgad', probs_b, value_f).astype(jnp.bfloat16))
    delta = jnp.einsum('tgad,tgad->gat', output.astype(jnp.float32), grad_f)[..., None]
    dprobs = jnp.einsum('tgad,gkd->gatk', grad_f, value_f)
    dscores = lax.optimization_barrier((probs * (dprobs - delta)).astype(jnp.bfloat16)).astype(jnp.float32)
    query_grad = (jnp.einsum('gatk,gkd->tgad', dscores, key_f) * scaling).astype(jnp.bfloat16)
    key_terms = jnp.einsum('gatk,tgad->gkd', dscores, query_f) * scaling
    value_terms = jnp.einsum('gatk,tgad->gkd', probs_b, grad_f)
    return (output, query_grad, key_terms, value_terms)

def assemble(local_blocks, slot_blocks, blocks_here, random_count):
    kv_local = local_blocks.shape[0]
    tail = slot_blocks.shape[2:]
    extended = jnp.concatenate([slot_blocks[:, 0:1], local_blocks, slot_blocks[:, 1:2]], axis=1)
    window_part = jnp.stack([extended[:, offset:offset + blocks_here] for offset in range(3)], axis=2)
    global_part = jnp.broadcast_to(slot_blocks[:, None, 2:4], (kv_local, blocks_here, 2) + tail)
    random_part = slot_blocks[:, 4:].reshape((kv_local, blocks_here, random_count) + tail)
    joined = jnp.concatenate([window_part, global_part, random_part], axis=2)
    return joined.reshape(kv_local, blocks_here, -1, tail[-1]).transpose(1, 0, 2, 3)

def spread(parts, blocks_here, block_len, random_count):
    kv_local = parts.shape[1]
    head_dim = parts.shape[-1]
    parts = parts.reshape(blocks_here, kv_local, 5 + random_count, block_len, head_dim)
    moved = parts.transpose(1, 0, 2, 3, 4)
    extended = jnp.zeros((kv_local, blocks_here + 2, block_len, head_dim), moved.dtype)
    for offset in range(3):
        extended = extended.at[:, offset:offset + blocks_here].add(moved[:, :, offset])
    local_sum = extended[:, 1:blocks_here + 1]
    edge_sum = jnp.stack([extended[:, 0], extended[:, blocks_here + 1]], axis=1)
    global_sum = lax.optimization_barrier(jnp.sum(moved[:, :, 3:5], axis=1))
    random_sum = moved[:, :, 5:].reshape(kv_local, blocks_here * random_count, block_len, head_dim)
    return (local_sum, jnp.concatenate([edge_sum, global_sum, random_sum], axis=1))

def reference(queries, keys, values, out_grad, rand_blocks, global_blocks):
    shard_count = NB // QB
    scaling = 1.0 / math.sqrt(DH)
    key_all = keys.reshape(NB, BS, KVH, DH).transpose(2, 0, 1, 3)
    value_all = values.reshape(NB, BS, KVH, DH).transpose(2, 0, 1, 3)
    head_range = jnp.arange(KVH, dtype=jnp.int32)
    query_shards = queries.reshape(shard_count, QB, BS, KVH, GROUP, DH)
    grad_shards = out_grad.reshape(shard_count, QB, BS, KVH, GROUP, DH)
    rand_shards = rand_blocks.reshape(shard_count, QB, KVH, RAND)
    shard_ids = jnp.arange(shard_count, dtype=jnp.int32)

    def shard_step(carry, inputs):
        key_total, value_total = carry
        index, query_shard, grad_shard, rand_shard = inputs
        start = (index * QB).astype(jnp.int32)
        left_edge = (start - 1) % NB
        right_edge = (start + QB) % NB
        edge_ids = jnp.broadcast_to(jnp.stack([left_edge, right_edge]).astype(jnp.int32)[None, :], (KVH, 2))
        global_ids = jnp.broadcast_to(global_blocks.astype(jnp.int32)[None, :], (KVH, 2))
        random_ids = rand_shard.transpose(1, 0, 2).reshape(KVH, QB * RAND).astype(jnp.int32)
        slot_ids = jnp.concatenate([edge_ids, global_ids, random_ids], axis=1)
        slot_keys = key_all[head_range[:, None], slot_ids]
        slot_values = value_all[head_range[:, None], slot_ids]
        local_keys = lax.dynamic_slice_in_dim(key_all, start, QB, 1)
        local_values = lax.dynamic_slice_in_dim(value_all, start, QB, 1)
        key_sets = assemble(local_keys, slot_keys, QB, RAND)
        value_sets = assemble(local_values, slot_values, QB, RAND)

        def one_block(pieces):
            return attend_rows(pieces[0], pieces[1], pieces[2], pieces[3], scaling)
        output, query_grad, key_terms, value_terms = lax.map(one_block, (query_shard, key_sets, value_sets, grad_shard))
        local_k, slot_k = spread(key_terms, QB, BS, RAND)
        local_v, slot_v = spread(value_terms, QB, BS, RAND)
        slot_k = lax.optimization_barrier(slot_k.astype(jnp.bfloat16)).astype(jnp.float32)
        slot_v = lax.optimization_barrier(slot_v.astype(jnp.bfloat16)).astype(jnp.float32)
        key_total = lax.dynamic_update_slice_in_dim(key_total, lax.dynamic_slice_in_dim(key_total, start, QB, 1) + local_k, start, 1)
        value_total = lax.dynamic_update_slice_in_dim(value_total, lax.dynamic_slice_in_dim(value_total, start, QB, 1) + local_v, start, 1)
        key_total = key_total.at[head_range[:, None], slot_ids].add(slot_k)
        value_total = value_total.at[head_range[:, None], slot_ids].add(slot_v)
        return ((key_total, value_total), (output, query_grad))
    zeros = jnp.zeros((KVH, NB, BS, DH), jnp.float32)
    totals, outputs = lax.scan(shard_step, (zeros, zeros), (shard_ids, query_shards, grad_shards, rand_shards))
    attn_out = outputs[0].reshape(SEQ, HQ, DH)
    query_grad = outputs[1].reshape(SEQ, HQ, DH)
    key_grad = totals[0].transpose(1, 2, 0, 3).reshape(SEQ, KVH, DH).astype(jnp.bfloat16)
    value_grad = totals[1].transpose(1, 2, 0, 3).reshape(SEQ, KVH, DH).astype(jnp.bfloat16)
    return (attn_out, query_grad, key_grad, value_grad)
```

```python
import functools
import math

import jax
import jax.numpy as jnp
from jax import lax
from jax.experimental import pallas as pl
from jax.experimental.pallas import tpu as pltpu
from jax.sharding import PartitionSpec as P

MESH = pl.DeviceIdType.MESH
NY, NZ, NH = 4, 8, 8
QB, BS, DH, RAND = 6, 128, 128, 3
ROWS = QB * BS
PART = ROWS // NH
LIST = 8 * BS
CHUNK = 256
SLOTS = QB * RAND
SCALE = 1.0 / math.sqrt(DH)
LOG2E = 1.4426950408889634
F32, BF16 = jnp.float32, jnp.bfloat16

T_WANT, T_PICK, T_OWN, T_SLOT, T_GLOB = 0, 32, 64, 82, 114


def dot(a, b, dims):
    return lax.dot_general(a, b, (dims, ((), ())), preferred_element_type=F32)


def flag(a, b):
    return (a == b).astype(jnp.int32).astype(F32)


def body(
    tab, q_s, g_s, kv_s, o_out, dq_out, dkv_out,
    qh, gh, r0, rp1, rp2, rp3, rm1, rm2, rm3, r4, xs, xr, edge, gs, gr,
    lk, lv, lkt, lvt, ob, dqb, awk, awv, agk, agv, ark, arv,
    ys, yr, es, er, gs2, gr2, part, ssp, ssm, srp, srm, dkvb,
    head_ss, head_rs, q_ss, q_rs, g_ss, g_rs, loc,
    zp_ss, zp_rs, zm_ss, zm_rs, e_ss, e_rs, y_ss, y_rs, gl_ss, gl_rs,
    o_ss, o_rs, dq_ss, dq_rs, w_ss, w_rs, e2_ss, e2_rs, gl2_ss, gl2_rs,
    pp_ss, pp_rs, pm_ss, pm_rs, dkv_ss, dkv_rs,
):
    blk = lax.axis_index("blk")
    head = lax.axis_index("head")
    y, z = blk // NZ, blk % NZ
    x = head // 2
    up = (y * NZ + (z + 1) % NZ, head)
    down = (y * NZ + (z + NZ - 1) % NZ, head)
    after = ((blk + 1) % (NY * NZ), head)
    before = ((blk + NY * NZ - 1) % (NY * NZ), head)

    def column(dy):
        return (((y + dy) % NY) * NZ + z, head)

    def remote(src, dst, ss, rs, dev):
        return pltpu.make_async_remote_copy(
            src_ref=src, dst_ref=dst, send_sem=ss, recv_sem=rs, device_id=dev, device_id_type=MESH
        )

    bar = pltpu.get_barrier_semaphore()

    def greet(dev):
        pl.semaphore_signal(bar, inc=1, device_id=dev, device_id_type=MESH)

    def greet_head(k, c):
        greet((blk, (head + k) % NH))
        return c

    lax.fori_loop(1, NH, greet_head, 0)
    for dev in (up, down, after, before):
        greet(dev)
    for dy in range(1, NY):
        greet(column(dy))
    pl.semaphore_wait(bar, NH - 1 + 4 + NY - 1)

    mine = pl.ds(pl.multiple_of(head * PART, 32), PART)
    rows_mine = pl.ds(pl.multiple_of(head * ROWS, 256), ROWS)

    def kv_copy(h):
        return remote(kv_s.at[h], r0.at[:, mine, :], head_ss.at[h], head_rs.at[head], (blk, h))

    def kv_arrival(h):
        there = pl.ds(pl.multiple_of(h * PART, 32), PART)
        return remote(kv_s.at[h], r0.at[:, there, :], head_ss.at[h], head_rs.at[h], (blk, h))

    def q_copy(h):
        return remote(q_s.at[h], qh.at[rows_mine, :], q_ss.at[h], q_rs.at[head], (blk, h))

    def g_copy(h):
        return remote(g_s.at[h], gh.at[rows_mine, :], g_ss.at[h], g_rs.at[head], (blk, h))

    def q_arrival(h):
        there = pl.ds(pl.multiple_of(h * ROWS, 256), ROWS)
        return remote(q_s.at[h], qh.at[there, :], q_ss.at[h], q_rs.at[h], (blk, h))

    def g_arrival(h):
        there = pl.ds(pl.multiple_of(h * ROWS, 256), ROWS)
        return remote(g_s.at[h], gh.at[there, :], g_ss.at[h], g_rs.at[h], (blk, h))

    own_kv = pltpu.make_async_copy(kv_s.at[head], r0.at[:, mine, :], loc.at[0])
    own_q = pltpu.make_async_copy(q_s.at[head], qh.at[rows_mine, :], loc.at[1])
    own_g = pltpu.make_async_copy(g_s.at[head], gh.at[rows_mine, :], loc.at[2])
    own_kv.start()

    def send_kv(k, c):
        kv_copy((head + k) % NH).start()
        return c

    def send_qg(k, c):
        h = (head + k) % NH
        q_copy(h).start()
        g_copy(h).start()
        return c

    lax.fori_loop(1, NH, send_kv, 0)
    own_q.start()
    own_g.start()
    lax.fori_loop(1, NH, send_qg, 0)

    zero = jnp.zeros((BS, DH), F32)
    for ref in (awk, awv, agk, agv, ark, arv):
        def clear(n, c, ref=ref):
            ref[pl.ds(pl.multiple_of(n * BS, BS), BS), :] = zero
            return c
        lax.fori_loop(0, ref.shape[0] // BS, clear, 0)

    own_kv.wait()

    def wait_kv(k, c):
        kv_arrival((head + k) % NH).wait_recv()
        return c

    lax.fori_loop(1, NH, wait_kv, 0)

    plus = [r0, rp1, rp2, rp3, r4]
    minus = [r0, rm1, rm2, rm3, r4]

    def z_copy(step, half, upward):
        chain = plus if upward else minus
        ss, rs = (zp_ss, zp_rs) if upward else (zm_ss, zm_rs)
        return remote(
            chain[step].at[half], chain[step + 1].at[half],
            ss.at[step, half], rs.at[step, half], up if upward else down,
        )

    to_after = remote(r0.at[:, pl.ds(ROWS - BS, BS), :], edge.at[0], e_ss.at[0], e_rs.at[0], after)
    to_before = remote(r0.at[:, pl.ds(0, BS), :], edge.at[1], e_ss.at[1], e_rs.at[1], before)
    for half in (0, 1):
        z_copy(0, half, True).start()
        z_copy(0, half, False).start()
    to_after.start()
    to_before.start()

    glob = [tab[T_GLOB + j] for j in range(2)]
    g_within = [tab[T_GLOB + 2 + j] for j in range(2)]
    g_z = [tab[T_GLOB + 4 + j] for j in range(2)]
    g_y = [tab[T_GLOB + 6 + j] for j in range(2)]

    def block_rows(w):
        return pl.ds(w * BS, BS)

    def y_copy(dy, index, shard_z):
        dev = column(dy)
        return remote(
            xs.at[index * 4 + dy], xr.at[y * NZ + shard_z],
            y_ss.at[index, dy], y_rs.at[index, (NY - dy) % NY], dev,
        )

    def y_arrival(dy, index, shard_z):
        return remote(
            xs.at[index * 4 + dy], xr.at[((y + dy) % NY) * NZ + shard_z],
            y_ss.at[index, dy], y_rs.at[index, dy], column(dy),
        )

    order = [(r0, 0), (rp1, -1), (rm1, 1), (rp2, -2), (rm2, 2), (rp3, -3), (rm3, 3), (r4, 4)]

    def shard_of(delta):
        return (z + delta + NZ) % NZ

    def serve(index):
        buf, delta = order[index]
        sz = shard_of(delta)

        def one(dy, c):
            w = tab[T_PICK + ((y + dy) % NY) * NZ + sz]
            xs[index * 4 + dy] = buf[:, block_rows(w), :]
            y_copy(dy, index, sz).start()
            return c

        lax.fori_loop(1, NY, one, 0)
        w = tab[T_PICK + y * NZ + sz]
        xr[y * NZ + sz] = buf[:, block_rows(w), :]
        for j in range(2):
            picked = buf[:, block_rows(g_within[j]), :]
            kept = picked.astype(F32) * flag(g_z[j], sz)
            if index == 0:
                gs[j] = kept.astype(BF16)
            else:
                gs[j] = (gs[j].astype(F32) + kept).astype(BF16)

    serve(0)
    for step in (1, 2, 3):
        for half in (0, 1):
            z_copy(step - 1, half, True).wait_recv()
            if step < 3 or half == 0:
                z_copy(step, half, True).start()
            z_copy(step - 1, half, False).wait_recv()
            if step < 3 or half == 1:
                z_copy(step, half, False).start()
        serve(2 * step - 1)
        serve(2 * step)
    z_copy(3, 0, True).wait_recv()
    z_copy(3, 1, False).wait_recv()
    serve(7)

    def gl_copy(dy):
        return remote(gs, gr.at[y], gl_ss.at[dy], gl_rs.at[NY - dy], column(dy))

    def gl_arrival(dy):
        return remote(gs, gr.at[(y + dy) % NY], gl_ss.at[dy], gl_rs.at[dy], column(dy))

    for dy in range(1, NY):
        gl_copy(dy).start()
    gr[y] = gs[...]

    to_after.wait_recv()
    to_before.wait_recv()

    def place(i, s, kb, vb, kt, vt):
        lk[i, s * BS:(s + 1) * BS, :] = kb
        lv[i, s * BS:(s + 1) * BS, :] = vb
        lkt[i, :, s * BS:(s + 1) * BS] = kt
        lvt[i, :, s * BS:(s + 1) * BS] = vt

    def turned(block):
        return block.astype(F32).T.astype(BF16)

    for e in range(QB + 2):
        if e == 0:
            kb, vb = edge[0, 0], edge[0, 1]
        elif e == QB + 1:
            kb, vb = edge[1, 0], edge[1, 1]
        else:
            kb, vb = r0[0, (e - 1) * BS:e * BS, :], r0[1, (e - 1) * BS:e * BS, :]
        kt, vt = turned(kb), turned(vb)
        for s in range(3):
            if 0 <= e - s < QB:
                place(e - s, s, kb, vb, kt, vt)

    for dy in range(1, NY):
        gl_arrival(dy).wait_recv()
    for j in range(2):
        kb, vb = gr[g_y[j], j, 0], gr[g_y[j], j, 1]
        kt, vt = turned(kb), turned(vb)
        for i in range(QB):
            place(i, 3 + j, kb, vb, kt, vt)

    for index in range(8):
        def wait_y(dy, c, index=index):
            y_arrival(dy, index, shard_of(order[index][1])).wait_recv()
            return c
        lax.fori_loop(1, NY, wait_y, 0)

    def place_random(i, c):
        for r in range(RAND):
            owner = tab[T_OWN + i * RAND + r]
            kb, vb = xr[owner, 0], xr[owner, 1]
            place(i, 5 + r, kb, vb, turned(kb), turned(vb))
        return c

    lax.fori_loop(0, QB, place_random, 0)

    own_q.wait()
    own_g.wait()

    def wait_qg(k, c):
        h = (head + k) % NH
        q_arrival(h).wait_recv()
        g_arrival(h).wait_recv()
        return c

    lax.fori_loop(1, NH, wait_qg, 0)

    def attend(j):
        rows = pl.ds(pl.multiple_of(j * CHUNK, CHUNK), CHUNK)
        i = j // 4
        q = qh[rows, :]
        g = gh[rows, :]
        st = dot(lk[i], q, ((1,), (1,)))
        peak = jnp.max(st, axis=0, keepdims=True)
        ex = jnp.exp2((st - peak) * (SCALE * LOG2E))
        inv = 1.0 / jnp.sum(ex, axis=0, keepdims=True)
        pt = ex * inv
        pb = pt.astype(BF16)
        ot = dot(lvt[i], pb, ((1,), (0,)))
        o = ot.T.astype(BF16)
        ob[rows, :] = o
        gt = g.astype(F32).T
        delta = jnp.sum(ot.astype(BF16).astype(F32) * gt, axis=0, keepdims=True)
        dpt = dot(lv[i], g, ((1,), (1,)))
        ds = (pt * (dpt - delta)).astype(BF16)
        dqt = dot(lkt[i], ds, ((1,), (0,))) * SCALE
        dqb[rows, :] = dqt.T.astype(BF16)
        dv = dot(pb, g, ((1,), (0,)))
        dk = dot(ds, q, ((1,), (0,)))
        base = pl.multiple_of(i * BS, BS)
        rbase = pl.multiple_of(i * RAND * BS, BS)
        awk[pl.ds(base, 3 * BS), :] += dk[0:3 * BS]
        awv[pl.ds(base, 3 * BS), :] += dv[0:3 * BS]
        agk[...] += dk[3 * BS:5 * BS]
        agv[...] += dv[3 * BS:5 * BS]
        ark[pl.ds(rbase, RAND * BS), :] += dk[5 * BS:]
        arv[pl.ds(rbase, RAND * BS), :] += dv[5 * BS:]

    def there_rows(h):
        return pl.ds(pl.multiple_of(h * ROWS, 256), ROWS)

    def o_copy(h):
        return remote(ob.at[there_rows(h), :], o_out.at[head], o_ss.at[h], o_rs.at[head], (blk, h))

    def dq_copy(h):
        return remote(dqb.at[there_rows(h), :], dq_out.at[head], dq_ss.at[h], dq_rs.at[head], (blk, h))

    def o_arrival(h):
        return remote(ob.at[there_rows(h), :], o_out.at[h], o_ss.at[h], o_rs.at[h], (blk, h))

    def dq_arrival(h):
        return remote(dqb.at[there_rows(h), :], dq_out.at[h], dq_ss.at[h], dq_rs.at[h], (blk, h))

    own_o = pltpu.make_async_copy(ob.at[there_rows(head), :], o_out.at[head], loc.at[3])
    own_dq = pltpu.make_async_copy(dqb.at[there_rows(head), :], dq_out.at[head], loc.at[4])

    def attend_part(n, c):
        h = (2 * x + 2 + n) % NH

        def chunk(t, cc):
            attend(h * 3 + t)
            return cc

        lax.fori_loop(0, 3, chunk, 0)

        @pl.when(h != head)
        def _():
            o_copy(h).start()
            dq_copy(h).start()

        return c

    lax.fori_loop(0, NH, attend_part, 0)
    own_o.start()
    own_dq.start()

    out_edge = [0, QB + 1]
    for n in range(2):
        rows = slice(out_edge[n] * BS, (out_edge[n] + 1) * BS)
        es[n, 0] = (awk[rows, :] * SCALE).astype(BF16)
        es[n, 1] = awv[rows, :].astype(BF16)
    e2_before = remote(es.at[0], er.at[1], e2_ss.at[0], e2_rs.at[1], before)
    e2_after = remote(es.at[1], er.at[0], e2_ss.at[1], e2_rs.at[0], after)
    e2_before.start()
    e2_after.start()

    gs2[0] = (agk[...] * SCALE).astype(BF16)
    gs2[1] = agv[...].astype(BF16)

    def gl2_copy(dy):
        return remote(gs2, gr2.at[y], gl2_ss.at[dy], gl2_rs.at[NY - dy], column(dy))

    def gl2_arrival(dy):
        return remote(gs2, gr2.at[(y + dy) % NY], gl2_ss.at[dy], gl2_rs.at[dy], column(dy))

    for dy in range(1, NY):
        gl2_copy(dy).start()
    gr2[y] = gs2[...]

    def w_copy(dy, index):
        return remote(
            ys.at[index * 4 + dy], yr.at[index * 4 + y],
            w_ss.at[index, dy], w_rs.at[index, (NY - dy) % NY], column(dy),
        )

    def w_arrival(dy, index):
        return remote(
            ys.at[index * 4 + dy], yr.at[index * 4 + (y + dy) % NY],
            w_ss.at[index, dy], w_rs.at[index, dy], column(dy),
        )

    back = [4, 3, -3, 2, -2, 1, -1, 0]

    def slot_rows(slot):
        return pl.ds(slot * BS, BS)

    for index, delta in enumerate(back):
        sz = shard_of(delta)

        def give(dy, c, index=index, sz=sz):
            slot = tab[T_SLOT + ((y + dy) % NY) * NZ + sz]
            ys[index * 4 + dy, 0] = (ark[slot_rows(slot), :] * SCALE).astype(BF16)
            ys[index * 4 + dy, 1] = arv[slot_rows(slot), :].astype(BF16)
            w_copy(dy, index).start()
            return c

        lax.fori_loop(1, NY, give, 0)
        slot = tab[T_SLOT + y * NZ + sz]
        yr[index * 4 + y, 0] = (ark[slot_rows(slot), :] * SCALE).astype(BF16)
        yr[index * 4 + y, 1] = arv[slot_rows(slot), :].astype(BF16)

    for dy in range(1, NY):
        gl2_arrival(dy).wait_recv()

    def add_up(index):
        sz = shard_of(back[index])

        def wait_w(dy, c):
            w_arrival(dy, index).wait_recv()
            return c

        lax.fori_loop(1, NY, wait_w, 0)

        def one_block(b, c):
            for half in range(2):
                total = jnp.zeros((BS, DH), F32)
                for yy in range(NY):
                    hit = flag(tab[T_WANT + yy * NZ + sz], b)
                    total += yr[index * 4 + yy, half].astype(F32) * hit
                for j in range(2):
                    hit = flag(glob[j], (y * NZ + sz) * QB + b)
                    summed = jnp.zeros((BS, DH), F32)
                    for yy in range(NY):
                        summed += gr2[yy, half, j * BS:(j + 1) * BS, :].astype(F32)
                    total += summed * hit
                part[half, pl.ds(pl.multiple_of(b * BS, BS), BS), :] = total
            return c

        lax.fori_loop(0, QB, one_block, 0)

    def p_copy(step, half, upward):
        if upward:
            return remote(ssp.at[step, half], srp.at[step, half], pp_ss.at[step, half], pp_rs.at[step, half], up)
        return remote(ssm.at[step, half], srm.at[step, half], pm_ss.at[step, half], pm_rs.at[step, half], down)

    add_up(0)
    ssp[0, 0] = part[0].astype(BF16)
    p_copy(0, 0, True).start()
    ssm[0, 1] = part[1].astype(BF16)
    p_copy(0, 1, False).start()
    for step in (1, 2, 3):
        for upward in (True, False):
            add_up(2 * step - 1 if upward else 2 * step)
            first = 0 if upward else 1
            send, recv = (ssp, srp) if upward else (ssm, srm)
            for half in (first, 1 - first):
                if step > 1 or half == first:
                    p_copy(step - 1, half, upward).wait_recv()
                    send[step, half] = (part[half] + recv[step - 1, half].astype(F32)).astype(BF16)
                else:
                    send[step, half] = part[half].astype(BF16)
                p_copy(step, half, upward).start()
    add_up(7)
    e2_before.wait_send()
    e2_after.wait_send()
    remote(es.at[0], er.at[1], e2_ss.at[0], e2_rs.at[1], before).wait_recv()
    remote(es.at[1], er.at[0], e2_ss.at[1], e2_rs.at[0], after).wait_recv()
    for half, window in ((0, awk), (1, awv)):
        factor = SCALE if half == 0 else 1.0
        p_copy(3, half, True).wait_recv()
        p_copy(3, half, False).wait_recv()
        for b in range(QB):
            rows = slice(b * BS, (b + 1) * BS)
            total = window[(b + 1) * BS:(b + 2) * BS, :] * factor + part[half, rows, :]
            total += srp[3, half, rows, :].astype(F32) + srm[3, half, rows, :].astype(F32)
            if b == 0:
                total += er[0, half].astype(F32)
            if b == QB - 1:
                total += er[1, half].astype(F32)
            dkvb[half, rows, :] = total.astype(BF16)

    def part_rows(h):
        return pl.ds(pl.multiple_of(h * PART, 32), PART)

    def dkv_copy(h):
        return remote(dkvb.at[:, part_rows(h), :], dkv_out.at[head], dkv_ss.at[h], dkv_rs.at[head], (blk, h))

    def dkv_arrival(h):
        return remote(dkvb.at[:, part_rows(h), :], dkv_out.at[h], dkv_ss.at[h], dkv_rs.at[h], (blk, h))

    own_dkv = pltpu.make_async_copy(dkvb.at[:, mine, :], dkv_out.at[head], loc.at[5])

    def send_dkv(k, c):
        dkv_copy((head + k) % NH).start()
        return c

    lax.fori_loop(1, NH, send_dkv, 0)
    own_dkv.start()

    def drain(k, c):
        h = (head + k) % NH
        kv_copy(h).wait_send()
        q_copy(h).wait_send()
        g_copy(h).wait_send()
        o_copy(h).wait_send()
        dq_copy(h).wait_send()
        dkv_copy(h).wait_send()
        o_arrival(h).wait_recv()
        dq_arrival(h).wait_recv()
        dkv_arrival(h).wait_recv()
        return c

    for step in range(4):
        for half in range(2):
            if step < 3 or half == 0:
                z_copy(step, half, True).wait_send()
            if step < 3 or half == 1:
                z_copy(step, half, False).wait_send()
            if step > 0 or half == 0:
                p_copy(step, half, True).wait_send()
            if step > 0 or half == 1:
                p_copy(step, half, False).wait_send()
    to_after.wait_send()
    to_before.wait_send()

    def drain_column(dy, c):
        gl_copy(dy).wait_send()
        gl2_copy(dy).wait_send()
        for index in range(8):
            y_copy(dy, index, shard_of(order[index][1])).wait_send()
            w_copy(dy, index).wait_send()
        return c

    lax.fori_loop(1, NY, drain_column, 0)
    lax.fori_loop(1, NH, drain, 0)
    own_o.wait()
    own_dq.wait()
    own_dkv.wait()


def tables(rand_blocks, global_blocks):
    blk = lax.axis_index("blk")
    head = lax.axis_index("head")
    y, z = blk // NZ, blk % NZ
    chosen = lax.dynamic_slice_in_dim(rand_blocks, head, 1, 1).reshape(NY, NZ, SLOTS)
    column = lax.dynamic_slice_in_dim(chosen, z, 1, 1)
    owners = y * NZ + jnp.arange(NZ, dtype=jnp.int32)[None, :, None]
    want = jnp.max(jnp.where(column // QB == owners, column % QB, -1), axis=2)
    own = lax.dynamic_slice_in_dim(chosen.reshape(NY * NZ, SLOTS), blk, 1, 0)[0] // QB
    shards = jnp.arange(NY * NZ, dtype=jnp.int32)[:, None]
    slot = jnp.max(
        jnp.where(own[None, :] == shards, jnp.arange(SLOTS, dtype=jnp.int32)[None, :], 0), axis=1
    )
    want = want.reshape(-1)
    picked = jnp.maximum(want, 0)
    shard = global_blocks // QB
    return jnp.concatenate(
        [want, picked, own, slot, global_blocks, global_blocks % QB, shard % NZ, shard // NZ]
    )


def on_device(queries, keys, values, out_grad, rand_blocks, global_blocks):
    tab = tables(rand_blocks, global_blocks)
    heads = queries.shape[1] // NH
    q_s = queries.reshape(PART, NH, heads, DH).transpose(1, 0, 2, 3).reshape(NH, ROWS, DH)
    g_s = out_grad.reshape(PART, NH, heads, DH).transpose(1, 0, 2, 3).reshape(NH, ROWS, DH)
    kv_s = jnp.stack([keys, values]).transpose(2, 0, 1, 3)
    vm = lambda shape, dtype=BF16: pltpu.VMEM(shape, dtype)
    dma = lambda *shape: pltpu.SemaphoreType.DMA(shape)
    total = NH * ROWS
    pair = (2, BS, DH)
    anywhere = pl.BlockSpec(memory_space=pl.ANY)
    o_h, dq_h, dkv_h = pl.pallas_call(
        body,
        out_shape=(
            jax.ShapeDtypeStruct((NH, ROWS, DH), BF16),
            jax.ShapeDtypeStruct((NH, ROWS, DH), BF16),
            jax.ShapeDtypeStruct((NH, 2, PART, DH), BF16),
        ),
        in_specs=[pl.BlockSpec(memory_space=pltpu.SMEM), anywhere, anywhere, anywhere],
        out_specs=(anywhere, anywhere, anywhere),
        scratch_shapes=[
            vm((total, DH)), vm((total, DH)),
            *[vm((2, ROWS, DH)) for _ in range(8)],
            vm((32,) + pair), vm((32,) + pair), vm((2,) + pair), vm((2,) + pair), vm((NY, 2) + pair),
            vm((QB, LIST, DH)), vm((QB, LIST, DH)), vm((QB, DH, LIST)), vm((QB, DH, LIST)),
            vm((total, DH)), vm((total, DH)),
            vm(((QB + 2) * BS, DH), F32), vm(((QB + 2) * BS, DH), F32),
            vm((2 * BS, DH), F32), vm((2 * BS, DH), F32),
            vm((SLOTS * BS, DH), F32), vm((SLOTS * BS, DH), F32),
            vm((32,) + pair), vm((32,) + pair), vm((2,) + pair), vm((2,) + pair),
            vm((2, 2 * BS, DH)), vm((NY, 2, 2 * BS, DH)),
            vm((2, ROWS, DH), F32),
            *[vm((4, 2, ROWS, DH)) for _ in range(4)],
            vm((2, ROWS, DH)),
            dma(NH), dma(NH), dma(NH), dma(NH), dma(NH), dma(NH), dma(6),
            dma(4, 2), dma(4, 2), dma(4, 2), dma(4, 2), dma(2), dma(2), dma(8, NY), dma(8, NY),
            dma(NY), dma(NY),
            dma(NH), dma(NH), dma(NH), dma(NH), dma(8, NY), dma(8, NY), dma(2), dma(2),
            dma(NY), dma(NY),
            dma(4, 2), dma(4, 2), dma(4, 2), dma(4, 2), dma(NH), dma(NH),
        ],
        compiler_params=pltpu.CompilerParams(
            collective_id=0, has_side_effects=True, vmem_limit_bytes=60 * 2**20
        ),
    )(tab, q_s, g_s, kv_s)

    def rows_back(part):
        return part.reshape(NH, PART, heads, DH).transpose(1, 0, 2, 3).reshape(PART, NH * heads, DH)

    kv_back = dkv_h.transpose(1, 2, 0, 3)
    return rows_back(o_h), rows_back(dq_h), kv_back[0], kv_back[1]


def solution(mesh):
    rows = P(("blk", "head"), None, None)
    return jax.shard_map(
        on_device,
        mesh=mesh,
        in_specs=(rows, rows, rows, rows, P(), P()),
        out_specs=(rows, rows, rows, rows),
        check_vma=False,
    )
```

```python
import functools
import math

import jax
import jax.numpy as jnp
from jax import lax
from jax.experimental import pallas as pl
from jax.experimental.pallas import tpu as pltpu
from jax.sharding import PartitionSpec as P

MESH = pl.DeviceIdType.MESH
NY, NZ, NH = 4, 8, 8
QB, BS, DH, RAND = 6, 128, 128, 3
ROWS = QB * BS
PART = ROWS // NH
LIST = 8 * BS
CHUNK = 256
NEAR, FAR = 5 * BS, RAND * BS
CHUNKS = NH * ROWS // CHUNK
PIECE = BS // NZ
SLOTS = QB * RAND
SCALE = 1.0 / math.sqrt(DH)
LOG2E = 1.4426950408889634
F32, BF16 = jnp.float32, jnp.bfloat16

T_WANT, T_PICK, T_OWN, T_SLOT, T_GLOB = 0, 32, 64, 82, 114


def dot(a, b, dims):
    return lax.dot_general(a, b, (dims, ((), ())), preferred_element_type=F32)


def flag(a, b):
    return (a == b).astype(jnp.int32).astype(F32)


def body(
    tab, q_s, g_s, kv_s, o_out, dq_out, dkv_out,
    qh, gh, r0, rp1, rp2, rp3, rm1, rm2, rm3, r4, xs, xr, edge,
    lkn, lvn, lktn, lvtn, lkf, lvf, lktf, lvtf, exn, dsf, o1, stats, ob, dqb,
    awk, awv, agk, agv, ark, arv,
    ys, yr, es, er, partp, partm, ssp, ssm, srp, srm, dkvb,
    ga, gy, gp, gz, gm, gf, gall,
    head_ss, head_rs, q_ss, q_rs, g_ss, g_rs, loc,
    zp_ss, zp_rs, zm_ss, zm_rs, e_ss, e_rs, y_ss, y_rs,
    a0_ss, a0_rs, a1_ss, a1_rs, a2_ss, a2_rs, a3_ss, a3_rs,
    o_ss, o_rs, dq_ss, dq_rs, w_ss, w_rs, e2_ss, e2_rs,
    pp_ss, pp_rs, pm_ss, pm_rs, dkv_ss, dkv_rs,
):
    blk = lax.axis_index("blk")
    head = lax.axis_index("head")
    y, z = blk // NZ, blk % NZ
    x, core = head // 2, head % 2
    up = (y * NZ + (z + 1) % NZ, head)
    down = (y * NZ + (z + NZ - 1) % NZ, head)
    after = ((blk + 1) % (NY * NZ), head)
    before = ((blk + NY * NZ - 1) % (NY * NZ), head)

    def column(dy):
        return (((y + dy) % NY) * NZ + z, head)

    def ring(dz):
        return (y * NZ + (z + dz) % NZ, head)

    def peer(k):
        t = k // 2
        return ((x + t * (t + 1) // 2) % (NH // 2)) * 2 + (core + k) % 2

    def remote(src, dst, ss, rs, dev):
        return pltpu.make_async_remote_copy(
            src_ref=src, dst_ref=dst, send_sem=ss, recv_sem=rs, device_id=dev, device_id_type=MESH
        )

    bar = pltpu.get_barrier_semaphore()

    def greet(dev):
        pl.semaphore_signal(bar, inc=1, device_id=dev, device_id_type=MESH)

    def greet_head(k, c):
        greet((blk, (head + k) % NH))
        return c

    lax.fori_loop(1, NH, greet_head, 0)
    for dev in (after, before):
        greet(dev)
    for dy in range(1, NY):
        greet(column(dy))

    def greet_ring(dz, c):
        greet(ring(dz))
        return c

    lax.fori_loop(1, NZ, greet_ring, 0)
    pl.semaphore_wait(bar, NH - 1 + 2 + NY - 1 + NZ - 1)

    mine = pl.ds(pl.multiple_of(head * PART, 32), PART)
    rows_mine = pl.ds(pl.multiple_of(head * ROWS, 256), ROWS)

    def kv_copy(h):
        return remote(kv_s.at[h], r0.at[:, mine, :], head_ss.at[h], head_rs.at[head], (blk, h))

    def kv_arrival(h):
        there = pl.ds(pl.multiple_of(h * PART, 32), PART)
        return remote(kv_s.at[h], r0.at[:, there, :], head_ss.at[h], head_rs.at[h], (blk, h))

    def q_copy(h):
        return remote(q_s.at[h], qh.at[rows_mine, :], q_ss.at[h], q_rs.at[head], (blk, h))

    def g_copy(h):
        return remote(g_s.at[h], gh.at[rows_mine, :], g_ss.at[h], g_rs.at[head], (blk, h))

    def q_arrival(h):
        there = pl.ds(pl.multiple_of(h * ROWS, 256), ROWS)
        return remote(q_s.at[h], qh.at[there, :], q_ss.at[h], q_rs.at[h], (blk, h))

    def g_arrival(h):
        there = pl.ds(pl.multiple_of(h * ROWS, 256), ROWS)
        return remote(g_s.at[h], gh.at[there, :], g_ss.at[h], g_rs.at[h], (blk, h))

    own_kv = pltpu.make_async_copy(kv_s.at[head], r0.at[:, mine, :], loc.at[0])
    own_q = pltpu.make_async_copy(q_s.at[head], qh.at[rows_mine, :], loc.at[1])
    own_g = pltpu.make_async_copy(g_s.at[head], gh.at[rows_mine, :], loc.at[2])
    own_kv.start()

    def send_kv(k, c):
        kv_copy(peer(k)).start()
        return c

    def send_q(k, c):
        q_copy(peer(k)).start()
        return c

    def send_g(k, c):
        g_copy(peer(k)).start()
        return c

    lax.fori_loop(1, NH, send_kv, 0)
    own_q.start()
    own_g.start()
    lax.fori_loop(1, NH, send_q, 0)
    lax.fori_loop(1, NH, send_g, 0)

    zero = jnp.zeros((BS, DH), F32)
    for ref in (awk, awv, agk, agv, ark, arv):
        def clear(n, c, ref=ref):
            ref[pl.ds(pl.multiple_of(n * BS, BS), BS), :] = zero
            return c
        lax.fori_loop(0, ref.shape[0] // BS, clear, 0)

    own_kv.wait()

    def wait_kv(k, c):
        kv_arrival((head + k) % NH).wait_recv()
        return c

    lax.fori_loop(1, NH, wait_kv, 0)

    plus = [r0, rp1, rp2, rp3, r4]
    minus = [r0, rm1, rm2, rm3, r4]

    def z_copy(step, half, upward):
        chain = plus if upward else minus
        ss, rs = (zp_ss, zp_rs) if upward else (zm_ss, zm_rs)
        return remote(
            chain[step].at[half], chain[step + 1].at[half],
            ss.at[step, half], rs.at[step, half], up if upward else down,
        )

    to_after = remote(r0.at[:, pl.ds(ROWS - BS, BS), :], edge.at[0], e_ss.at[0], e_rs.at[0], after)
    to_before = remote(r0.at[:, pl.ds(0, BS), :], edge.at[1], e_ss.at[1], e_rs.at[1], before)
    for half in (0, 1):
        z_copy(0, half, True).start()
        z_copy(0, half, False).start()
    to_after.start()
    to_before.start()

    glob = [tab[T_GLOB + j] for j in range(2)]
    g_within = [tab[T_GLOB + 2 + j] for j in range(2)]

    def ar_y(n, dy):
        return remote(ga.at[n, (y + dy) % NY], gy.at[n, y], a0_ss.at[n, dy], a0_rs.at[n, NY - dy], column(dy))

    def ar_z(n, dz):
        rows = pl.ds(pl.multiple_of(((z + dz) % NZ) * PIECE, PIECE), PIECE)
        return remote(gp.at[n, rows, :], gz.at[n, z], a1_ss.at[n, dz], a1_rs.at[n, NZ - dz], ring(dz))

    z_rows = pl.ds(pl.multiple_of(z * PIECE, PIECE), PIECE)

    def ar_zback(n, dz):
        return remote(gm.at[n], gf.at[n, z_rows, :], a2_ss.at[n, dz], a2_rs.at[n, NZ - dz], ring(dz))

    def ar_yback(n, dy):
        return remote(gf.at[n], gall.at[n, y], a3_ss.at[n, dy], a3_rs.at[n, NY - dy], column(dy))

    def each(count, make, what):
        def one(d, c):
            copy = make(d)
            copy.start() if what == "start" else copy.wait_send()
            return c
        lax.fori_loop(1, count, one, 0)

    def ar_start(n):
        each(NY, functools.partial(ar_y, n), "start")
        gy[n, y] = ga[n, y]

    def ar_one(n):
        for dy in range(1, NY):
            remote(ga.at[n, y], gy.at[n, (y + dy) % NY], a0_ss.at[n, dy], a0_rs.at[n, dy], column(dy)).wait_recv()
        total = gy[n, 0].astype(F32)
        for k in range(1, NY):
            total += gy[n, k].astype(F32)
        gp[n] = total.astype(BF16)
        each(NZ, functools.partial(ar_z, n), "start")
        gz[n, z] = gp[n, z_rows, :]

    def ar_two(n):
        for dz in range(1, NZ):
            remote(gm.at[n], gz.at[n, (z + dz) % NZ], a1_ss.at[n, dz], a1_rs.at[n, dz], ring(dz)).wait_recv()
        total = gz[n, 0].astype(F32)
        for k in range(1, NZ):
            total += gz[n, k].astype(F32)
        gm[n] = total.astype(BF16)
        each(NZ, functools.partial(ar_zback, n), "start")
        gf[n, z_rows, :] = gm[n]

    def ar_three(n):
        for dz in range(1, NZ):
            rows = pl.ds(pl.multiple_of(((z + dz) % NZ) * PIECE, PIECE), PIECE)
            remote(gm.at[n], gf.at[n, rows, :], a2_ss.at[n, dz], a2_rs.at[n, dz], ring(dz)).wait_recv()
        each(NY, functools.partial(ar_yback, n), "start")
        gall[n, y] = gf[n]

    def ar_end(n):
        for dy in range(1, NY):
            remote(gf.at[n], gall.at[n, (y + dy) % NY], a3_ss.at[n, dy], a3_rs.at[n, dy], column(dy)).wait_recv()

    def ar_drain(n):
        each(NY, functools.partial(ar_y, n), "wait")
        each(NZ, functools.partial(ar_z, n), "wait")
        each(NZ, functools.partial(ar_zback, n), "wait")
        each(NY, functools.partial(ar_yback, n), "wait")

    def block_rows(w):
        return pl.ds(w * BS, BS)

    def y_copy(dy, index, shard_z):
        dev = column(dy)
        return remote(
            xs.at[index * 4 + dy], xr.at[y * NZ + shard_z],
            y_ss.at[index, dy], y_rs.at[index, (NY - dy) % NY], dev,
        )

    def y_arrival(dy, index, shard_z):
        return remote(
            xs.at[index * 4 + dy], xr.at[((y + dy) % NY) * NZ + shard_z],
            y_ss.at[index, dy], y_rs.at[index, dy], column(dy),
        )

    order = [(r0, 0), (rp1, -1), (rm1, 1), (rp2, -2), (rm2, 2), (rp3, -3), (rm3, 3), (r4, 4)]

    def shard_of(delta):
        return (z + delta + NZ) % NZ

    def serve(index):
        buf, delta = order[index]
        sz = shard_of(delta)

        def one(dy, c):
            w = tab[T_PICK + ((y + dy) % NY) * NZ + sz]
            xs[index * 4 + dy] = buf[:, block_rows(w), :]
            y_copy(dy, index, sz).start()
            return c

        lax.fori_loop(1, NY, one, 0)
        w = tab[T_PICK + y * NZ + sz]
        xr[y * NZ + sz] = buf[:, block_rows(w), :]
    def place(i, s, kb, vb):
        if s < 5:
            k_list, v_list, kt_list, vt_list, at = lkn, lvn, lktn, lvtn, s * BS
        else:
            k_list, v_list, kt_list, vt_list, at = lkf, lvf, lktf, lvtf, (s - 5) * BS
        k_list[i, at:at + BS, :] = kb
        v_list[i, at:at + BS, :] = vb
        kt_list[i, :, at:at + BS] = turned(kb)
        vt_list[i, :, at:at + BS] = turned(vb)

    def turned(block):
        return block.astype(F32).T.astype(BF16)

    def place_window(e, kb, vb):
        for s in range(3):
            if 0 <= e - s < QB:
                place(e - s, s, kb, vb)

    def attend_near(j):
        rows = pl.ds(pl.multiple_of(j * CHUNK, CHUNK), CHUNK)
        i = j // 4
        q = qh[rows, :]
        st = dot(lkn[i], q, ((1,), (1,)))
        peak = jnp.max(st, axis=0, keepdims=True)
        ex = jnp.exp2((st - peak) * (SCALE * LOG2E))
        stats[j, 0:1, :] = peak
        stats[j, 1:2, :] = jnp.sum(ex, axis=0, keepdims=True)
        eb = ex.astype(BF16)
        exn[j] = eb
        o1[j] = dot(lvtn[i], eb, ((1,), (0,)))

    def attend_far(j):
        rows = pl.ds(pl.multiple_of(j * CHUNK, CHUNK), CHUNK)
        i = j // 4
        q = qh[rows, :]
        g = gh[rows, :]
        st = dot(lkf[i], q, ((1,), (1,)))
        dpt = dot(lvf[i], g, ((1,), (1,)))
        gt = g.astype(F32).T
        before_peak = stats[j, 0:1, :]
        peak = jnp.maximum(before_peak, jnp.max(st, axis=0, keepdims=True))
        shrink = jnp.exp2((before_peak - peak) * (SCALE * LOG2E))
        ex = jnp.exp2((st - peak) * (SCALE * LOG2E))
        inv = 1.0 / (shrink * stats[j, 1:2, :] + jnp.sum(ex, axis=0, keepdims=True))
        near = shrink * inv
        pt = ex * inv
        pb = pt.astype(BF16)
        ot = o1[j] * near + dot(lvtf[i], pb, ((1,), (0,)))
        ob[rows, :] = ot.T.astype(BF16)
        delta = jnp.sum(ot.astype(BF16).astype(F32) * gt, axis=0, keepdims=True)
        stats[j, 2:3, :] = near
        stats[j, 3:4, :] = delta
        ds = (pt * (dpt - delta)).astype(BF16)
        dsf[j] = ds
        rbase = pl.multiple_of(i * FAR, BS)
        arv[pl.ds(rbase, FAR), :] += dot(pb, g, ((1,), (0,)))
        ark[pl.ds(rbase, FAR), :] += dot(ds, q, ((1,), (0,)))

    def attend_back(j):
        rows = pl.ds(pl.multiple_of(j * CHUNK, CHUNK), CHUNK)
        i = j // 4
        q = qh[rows, :]
        g = gh[rows, :]
        dpt = dot(lvn[i], g, ((1,), (1,)))
        pt = exn[j].astype(F32) * stats[j, 2:3, :]
        pb = pt.astype(BF16)
        ds = (pt * (dpt - stats[j, 3:4, :])).astype(BF16)
        dqt = dot(lktn[i], ds, ((1,), (0,))) + dot(lktf[i], dsf[j], ((1,), (0,)))
        dqb[rows, :] = (dqt * SCALE).T.astype(BF16)
        dv = dot(pb, g, ((1,), (0,)))
        dk = dot(ds, q, ((1,), (0,)))
        base = pl.multiple_of(i * BS, BS)
        awk[pl.ds(base, 3 * BS), :] += dk[0:3 * BS]
        awv[pl.ds(base, 3 * BS), :] += dv[0:3 * BS]
        agk[...] += dk[3 * BS:]
        agv[...] += dv[3 * BS:]

    def three(h, what):
        def chunk(t, c):
            what(h * 3 + t)
            return c
        lax.fori_loop(0, 3, chunk, 0)

    def near_parts(first, last):
        def part(k, c):
            h = peer(k)

            @pl.when(k > 0)
            def _():
                q_arrival(h).wait_recv()

            three(h, attend_near)
            return c

        lax.fori_loop(first, last, part, 0)

    for j in range(2):
        here = flag(tab[T_GLOB + 4 + j], blk)
        for half in range(2):
            picked = r0[half, block_rows(g_within[j]), :].astype(F32)
            ga[0, 2 * j + half] = (picked * here).astype(BF16)
    ar_start(0)
    serve(0)
    for e in range(1, QB + 1):
        place_window(e, r0[0, (e - 1) * BS:e * BS, :], r0[1, (e - 1) * BS:e * BS, :])
    ar_one(0)

    def forward(step, half):
        z_copy(step - 1, half, True).wait_recv()
        if step < 3 or half == 0:
            z_copy(step, half, True).start()
        z_copy(step - 1, half, False).wait_recv()
        if step < 3 or half == 1:
            z_copy(step, half, False).start()

    forward(1, 0)
    ar_two(0)
    to_after.wait_recv()
    to_before.wait_recv()
    place_window(0, edge[0, 0], edge[0, 1])
    place_window(QB + 1, edge[1, 0], edge[1, 1])
    forward(1, 1)
    serve(1)
    serve(2)
    ar_three(0)
    forward(2, 0)
    ar_end(0)
    for j in range(2):
        for i in range(QB):
            place(i, 3 + j, gall[0, 2 * j], gall[0, 2 * j + 1])
    forward(2, 1)
    serve(3)
    serve(4)
    own_q.wait()
    near_parts(0, 2)
    forward(3, 0)
    near_parts(2, 4)
    forward(3, 1)
    serve(5)
    serve(6)
    near_parts(4, 6)
    z_copy(3, 0, True).wait_recv()
    z_copy(3, 1, False).wait_recv()
    serve(7)
    near_parts(6, 8)

    for index in range(8):
        def wait_y(dy, c, index=index):
            y_arrival(dy, index, shard_of(order[index][1])).wait_recv()
            return c
        lax.fori_loop(1, NY, wait_y, 0)

    def place_random(i, c):
        for r in range(RAND):
            owner = tab[T_OWN + i * RAND + r]
            place(i, 5 + r, xr[owner, 0], xr[owner, 1])
        return c

    lax.fori_loop(0, QB, place_random, 0)
    own_g.wait()

    def wait_g(k, c):
        g_arrival(peer(k)).wait_recv()
        return c

    lax.fori_loop(1, NH, wait_g, 0)

    def there_rows(h):
        return pl.ds(pl.multiple_of(h * ROWS, 256), ROWS)

    def o_copy(h):
        return remote(ob.at[there_rows(h), :], o_out.at[head], o_ss.at[h], o_rs.at[head], (blk, h))

    def dq_copy(h):
        return remote(dqb.at[there_rows(h), :], dq_out.at[head], dq_ss.at[h], dq_rs.at[head], (blk, h))

    def o_arrival(h):
        return remote(ob.at[there_rows(h), :], o_out.at[h], o_ss.at[h], o_rs.at[h], (blk, h))

    def dq_arrival(h):
        return remote(dqb.at[there_rows(h), :], dq_out.at[h], dq_ss.at[h], dq_rs.at[h], (blk, h))

    own_o = pltpu.make_async_copy(ob.at[there_rows(head), :], o_out.at[head], loc.at[3])
    own_dq = pltpu.make_async_copy(dqb.at[there_rows(head), :], dq_out.at[head], loc.at[4])

    def far_part(n, c):
        k = NH - 1 - n
        h = peer(k)
        three(h, attend_far)

        @pl.when(k > 0)
        def _():
            o_copy(h).start()

        return c

    lax.fori_loop(0, NH, far_part, 0)
    own_o.start()

    def back_parts(first, last):
        def part(n, c):
            k = NH - 1 - n
            h = peer(k)
            three(h, attend_back)

            @pl.when(k > 0)
            def _():
                dq_copy(h).start()

            return c

        lax.fori_loop(first, last, part, 0)

    def w_copy(dy, index):
        return remote(
            ys.at[index * 4 + dy], yr.at[index * 4 + y],
            w_ss.at[index, dy], w_rs.at[index, (NY - dy) % NY], column(dy),
        )

    def w_arrival(dy, index):
        return remote(
            ys.at[index * 4 + dy], yr.at[index * 4 + (y + dy) % NY],
            w_ss.at[index, dy], w_rs.at[index, dy], column(dy),
        )

    back = [4, 3, -3, 2, -2, 1, -1, 0]

    def slot_rows(slot):
        return pl.ds(slot * BS, BS)

    for index, delta in enumerate(back):
        sz = shard_of(delta)

        def give(dy, c, index=index, sz=sz):
            slot = tab[T_SLOT + ((y + dy) % NY) * NZ + sz]
            ys[index * 4 + dy, 0] = (ark[slot_rows(slot), :] * SCALE).astype(BF16)
            ys[index * 4 + dy, 1] = arv[slot_rows(slot), :].astype(BF16)
            w_copy(dy, index).start()
            return c

        lax.fori_loop(1, NY, give, 0)
        slot = tab[T_SLOT + y * NZ + sz]
        yr[index * 4 + y, 0] = (ark[slot_rows(slot), :] * SCALE).astype(BF16)
        yr[index * 4 + y, 1] = arv[slot_rows(slot), :].astype(BF16)

    def add_up(index, part):
        sz = shard_of(back[index])

        def wait_w(dy, c):
            w_arrival(dy, index).wait_recv()
            return c

        lax.fori_loop(1, NY, wait_w, 0)
        hits = [tab[T_WANT + yy * NZ + sz] for yy in range(NY)]

        def one_block(b, c):
            for half in range(2):
                total = yr[index * 4, half].astype(F32) * flag(hits[0], b)
                for yy in range(1, NY):
                    total += yr[index * 4 + yy, half].astype(F32) * flag(hits[yy], b)
                part[half, pl.ds(pl.multiple_of(b * BS, BS), BS), :] = total
            return c

        lax.fori_loop(0, QB, one_block, 0)

    def p_copy(step, half, upward):
        if upward:
            return remote(ssp.at[step, half], srp.at[step, half], pp_ss.at[step, half], pp_rs.at[step, half], up)
        return remote(ssm.at[step, half], srm.at[step, half], pm_ss.at[step, half], pm_rs.at[step, half], down)

    def pass_on(step):
        for waits in (False, True):
            for upward in (True, False):
                send, recv, part = (ssp, srp, partp) if upward else (ssm, srm, partm)
                first = 0 if upward else 1
                for half in (first, 1 - first):
                    if waits != (step > 1 or half == first):
                        continue
                    total = part[half]
                    if waits:
                        p_copy(step - 1, half, upward).wait_recv()
                        total += recv[step - 1, half].astype(F32)
                    send[step, half] = total.astype(BF16)
                    p_copy(step, half, upward).start()

    back_parts(0, 2)
    add_up(0, partp)
    ssp[0, 0] = partp[0].astype(BF16)
    p_copy(0, 0, True).start()
    ssm[0, 1] = partp[1].astype(BF16)
    p_copy(0, 1, False).start()
    back_parts(2, 4)
    add_up(1, partp)
    add_up(2, partm)
    pass_on(1)
    add_up(3, partp)
    add_up(4, partm)
    back_parts(4, 7)
    pass_on(2)
    add_up(5, partp)
    add_up(6, partm)
    back_parts(7, 8)
    own_dq.start()
    for n, at in ((0, 0), (1, QB + 1)):
        rows = slice(at * BS, (at + 1) * BS)
        es[n, 0] = (awk[rows, :] * SCALE).astype(BF16)
        es[n, 1] = awv[rows, :].astype(BF16)
    e2_before = remote(es.at[0], er.at[1], e2_ss.at[0], e2_rs.at[1], before)
    e2_after = remote(es.at[1], er.at[0], e2_ss.at[1], e2_rs.at[0], after)
    e2_before.start()
    e2_after.start()
    for j in range(2):
        rows = slice(j * BS, (j + 1) * BS)
        ga[1, 2 * j] = (agk[rows, :] * SCALE).astype(BF16)
        ga[1, 2 * j + 1] = agv[rows, :].astype(BF16)
    ar_start(1)
    pass_on(3)
    ar_one(1)
    add_up(7, partp)
    e2_before.wait_send()
    e2_after.wait_send()
    remote(es.at[0], er.at[1], e2_ss.at[0], e2_rs.at[1], before).wait_recv()
    remote(es.at[1], er.at[0], e2_ss.at[1], e2_rs.at[0], after).wait_recv()
    for half, window in ((0, awk), (1, awv)):
        factor = SCALE if half == 0 else 1.0
        for b in range(QB):
            rows = slice(b * BS, (b + 1) * BS)
            total = window[(b + 1) * BS:(b + 2) * BS, :] * factor + partp[half, rows, :]
            if b == 0:
                total += er[0, half].astype(F32)
            if b == QB - 1:
                total += er[1, half].astype(F32)
            partp[half, rows, :] = total
    ar_two(1)
    ar_three(1)
    ar_end(1)
    for half in range(2):
        p_copy(3, half, True).wait_recv()
        p_copy(3, half, False).wait_recv()
        for b in range(QB):
            rows = slice(b * BS, (b + 1) * BS)
            total = partp[half, rows, :]
            total += srp[3, half, rows, :].astype(F32) + srm[3, half, rows, :].astype(F32)
            for j in range(2):
                total += gall[1, 2 * j + half].astype(F32) * flag(glob[j], blk * QB + b)
            dkvb[half, rows, :] = total.astype(BF16)

    def part_rows(h):
        return pl.ds(pl.multiple_of(h * PART, 32), PART)

    def dkv_copy(h):
        return remote(dkvb.at[:, part_rows(h), :], dkv_out.at[head], dkv_ss.at[h], dkv_rs.at[head], (blk, h))

    def dkv_arrival(h):
        return remote(dkvb.at[:, part_rows(h), :], dkv_out.at[h], dkv_ss.at[h], dkv_rs.at[h], (blk, h))

    own_dkv = pltpu.make_async_copy(dkvb.at[:, mine, :], dkv_out.at[head], loc.at[5])

    def send_dkv(k, c):
        dkv_copy(peer(k)).start()
        return c

    lax.fori_loop(1, NH, send_dkv, 0)
    own_dkv.start()

    def drain(k, c):
        h = (head + k) % NH
        kv_copy(h).wait_send()
        q_copy(h).wait_send()
        g_copy(h).wait_send()
        o_copy(h).wait_send()
        dq_copy(h).wait_send()
        dkv_copy(h).wait_send()
        o_arrival(h).wait_recv()
        dq_arrival(h).wait_recv()
        dkv_arrival(h).wait_recv()
        return c

    for step in range(4):
        for half in range(2):
            if step < 3 or half == 0:
                z_copy(step, half, True).wait_send()
            if step < 3 or half == 1:
                z_copy(step, half, False).wait_send()
            if step > 0 or half == 0:
                p_copy(step, half, True).wait_send()
            if step > 0 or half == 1:
                p_copy(step, half, False).wait_send()
    to_after.wait_send()
    to_before.wait_send()

    def drain_column(dy, c):
        for index in range(8):
            y_copy(dy, index, shard_of(order[index][1])).wait_send()
            w_copy(dy, index).wait_send()
        return c

    lax.fori_loop(1, NY, drain_column, 0)
    ar_drain(0)
    ar_drain(1)
    lax.fori_loop(1, NH, drain, 0)
    own_o.wait()
    own_dq.wait()
    own_dkv.wait()


def tables(rand_blocks, global_blocks):
    blk = lax.axis_index("blk")
    head = lax.axis_index("head")
    y, z = blk // NZ, blk % NZ
    chosen = lax.dynamic_slice_in_dim(rand_blocks, head, 1, 1).reshape(NY, NZ, SLOTS)
    column = lax.dynamic_slice_in_dim(chosen, z, 1, 1)
    owners = y * NZ + jnp.arange(NZ, dtype=jnp.int32)[None, :, None]
    want = jnp.max(jnp.where(column // QB == owners, column % QB, -1), axis=2)
    own = lax.dynamic_slice_in_dim(chosen.reshape(NY * NZ, SLOTS), blk, 1, 0)[0] // QB
    shards = jnp.arange(NY * NZ, dtype=jnp.int32)[:, None]
    slot = jnp.max(
        jnp.where(own[None, :] == shards, jnp.arange(SLOTS, dtype=jnp.int32)[None, :], 0), axis=1
    )
    want = want.reshape(-1)
    picked = jnp.maximum(want, 0)
    shard = global_blocks // QB
    return jnp.concatenate(
        [want, picked, own, slot, global_blocks, global_blocks % QB, shard]
    )


def on_device(queries, keys, values, out_grad, rand_blocks, global_blocks):
    tab = tables(rand_blocks, global_blocks)
    heads = queries.shape[1] // NH
    q_s = queries.reshape(PART, NH, heads, DH).transpose(1, 0, 2, 3).reshape(NH, ROWS, DH)
    g_s = out_grad.reshape(PART, NH, heads, DH).transpose(1, 0, 2, 3).reshape(NH, ROWS, DH)
    kv_s = jnp.stack([keys, values]).transpose(2, 0, 1, 3)
    vm = lambda shape, dtype=BF16: pltpu.VMEM(shape, dtype)
    dma = lambda *shape: pltpu.SemaphoreType.DMA(shape)
    total = NH * ROWS
    pair = (2, BS, DH)
    anywhere = pl.BlockSpec(memory_space=pl.ANY)
    o_h, dq_h, dkv_h = pl.pallas_call(
        body,
        out_shape=(
            jax.ShapeDtypeStruct((NH, ROWS, DH), BF16),
            jax.ShapeDtypeStruct((NH, ROWS, DH), BF16),
            jax.ShapeDtypeStruct((NH, 2, PART, DH), BF16),
        ),
        in_specs=[pl.BlockSpec(memory_space=pltpu.SMEM), anywhere, anywhere, anywhere],
        out_specs=(anywhere, anywhere, anywhere),
        scratch_shapes=[
            vm((total, DH)), vm((total, DH)),
            *[vm((2, ROWS, DH)) for _ in range(8)],
            vm((32,) + pair), vm((32,) + pair), vm((2,) + pair),
            vm((QB, NEAR, DH)), vm((QB, NEAR, DH)), vm((QB, DH, NEAR)), vm((QB, DH, NEAR)),
            vm((QB, FAR, DH)), vm((QB, FAR, DH)), vm((QB, DH, FAR)), vm((QB, DH, FAR)),
            vm((CHUNKS, NEAR, CHUNK)), vm((CHUNKS, FAR, CHUNK)), vm((CHUNKS, DH, CHUNK), F32),
            vm((CHUNKS, 8, CHUNK), F32),
            vm((total, DH)), vm((total, DH)),
            vm(((QB + 2) * BS, DH), F32), vm(((QB + 2) * BS, DH), F32),
            vm((2 * BS, DH), F32), vm((2 * BS, DH), F32),
            vm((SLOTS * BS, DH), F32), vm((SLOTS * BS, DH), F32),
            vm((32,) + pair), vm((32,) + pair), vm((2,) + pair), vm((2,) + pair),
            vm((2, ROWS, DH), F32), vm((2, ROWS, DH), F32),
            *[vm((4, 2, ROWS, DH)) for _ in range(4)],
            vm((2, ROWS, DH)),
            vm((2, NY, BS, DH)), vm((2, NY, BS, DH)), vm((2, BS, DH)), vm((2, NZ, PIECE, DH)),
            vm((2, PIECE, DH)), vm((2, BS, DH)), vm((2, NY, BS, DH)),
            dma(NH), dma(NH), dma(NH), dma(NH), dma(NH), dma(NH), dma(6),
            dma(4, 2), dma(4, 2), dma(4, 2), dma(4, 2), dma(2), dma(2), dma(8, NY), dma(8, NY),
            dma(2, NY), dma(2, NY), dma(2, NZ), dma(2, NZ), dma(2, NZ), dma(2, NZ), dma(2, NY), dma(2, NY),
            dma(NH), dma(NH), dma(NH), dma(NH), dma(8, NY), dma(8, NY), dma(2), dma(2),
            dma(4, 2), dma(4, 2), dma(4, 2), dma(4, 2), dma(NH), dma(NH),
        ],
        compiler_params=pltpu.CompilerParams(
            collective_id=0, has_side_effects=True, vmem_limit_bytes=60 * 2**20
        ),
    )(tab, q_s, g_s, kv_s)

    def rows_back(part):
        return part.reshape(NH, PART, heads, DH).transpose(1, 0, 2, 3).reshape(PART, NH * heads, DH)

    kv_back = dkv_h.transpose(1, 2, 0, 3)
    return rows_back(o_h), rows_back(dq_h), kv_back[0], kv_back[1]


def solution(mesh):
    rows = P(("blk", "head"), None, None)
    return jax.shard_map(
        on_device,
        mesh=mesh,
        in_specs=(rows, rows, rows, rows, P(), P()),
        out_specs=(rows, rows, rows, rows),
        check_vma=False,
    )
```

```python
import functools
import math

import jax
import jax.numpy as jnp
from jax import lax
from jax.experimental import pallas as pl
from jax.experimental.pallas import tpu as pltpu
from jax.sharding import PartitionSpec as P

MESH = pl.DeviceIdType.MESH
NY, NZ, NH = 4, 8, 8
QB, BS, DH, RAND = 6, 128, 128, 3
ROWS = QB * BS
PART = ROWS // NH
LIST = 8 * BS
CHUNK = 256
NEAR, FAR = 5 * BS, RAND * BS
CHUNKS = NH * ROWS // CHUNK
PIECE = BS // NZ
SLOTS = QB * RAND
SCALE = 1.0 / math.sqrt(DH)
LOG2E = 1.4426950408889634
F32, BF16 = jnp.float32, jnp.bfloat16

T_WANT, T_PICK, T_OWN, T_SLOT, T_GLOB = 0, 32, 64, 82, 114


def dot(a, b, dims):
    return lax.dot_general(a, b, (dims, ((), ())), preferred_element_type=F32)


def flag(a, b):
    return (a == b).astype(jnp.int32).astype(F32)


def body(
    tab, q_s, g_s, kv_s, o_out, dq_out, dkv_out,
    qh, gh, r0, rp1, rp2, rp3, rm1, rm2, rm3, r4, xs, xr, edge,
    lkn, lvn, lktn, lvtn, lkf, lvf, lktf, lvtf, exn, dsf, o1, stats, ob, dqb,
    awk, awv, agk, agv, ark, arv,
    ys, yr, es, er, partp, partm, fin, ssp, ssm, srp, srm, dkvb,
    ga, gy, gp, gz, gm, gf, gall,
    head_ss, head_rs, q_ss, q_rs, g_ss, g_rs, loc,
    zp_ss, zp_rs, zm_ss, zm_rs, e_ss, e_rs, y_ss, y_rs,
    a0_ss, a0_rs, a1_ss, a1_rs, a2_ss, a2_rs, a3_ss, a3_rs,
    o_ss, o_rs, dq_ss, dq_rs, w_ss, w_rs, e2_ss, e2_rs,
    pp_ss, pp_rs, pm_ss, pm_rs, dkv_ss, dkv_rs,
):
    blk = lax.axis_index("blk")
    head = lax.axis_index("head")
    y, z = blk // NZ, blk % NZ
    x, core = head // 2, head % 2
    up = (y * NZ + (z + 1) % NZ, head)
    down = (y * NZ + (z + NZ - 1) % NZ, head)
    after = ((blk + 1) % (NY * NZ), head)
    before = ((blk + NY * NZ - 1) % (NY * NZ), head)

    def column(dy):
        return (((y + dy) % NY) * NZ + z, head)

    def ring(dz):
        return (y * NZ + (z + dz) % NZ, head)

    def peer(k):
        t = k // 2
        return ((x + t * (t + 1) // 2) % (NH // 2)) * 2 + (core + k) % 2

    def remote(src, dst, ss, rs, dev):
        return pltpu.make_async_remote_copy(
            src_ref=src, dst_ref=dst, send_sem=ss, recv_sem=rs, device_id=dev, device_id_type=MESH
        )

    bar = pltpu.get_barrier_semaphore()

    def greet(dev):
        pl.semaphore_signal(bar, inc=1, device_id=dev, device_id_type=MESH)

    def greet_head(k, c):
        greet((blk, (head + k) % NH))
        return c

    lax.fori_loop(1, NH, greet_head, 0)
    for dev in (after, before):
        greet(dev)
    for dy in range(1, NY):
        greet(column(dy))

    def greet_ring(dz, c):
        greet(ring(dz))
        return c

    lax.fori_loop(1, NZ, greet_ring, 0)
    pl.semaphore_wait(bar, NH - 1 + 2 + NY - 1 + NZ - 1)

    mine = pl.ds(pl.multiple_of(head * PART, 32), PART)
    rows_mine = pl.ds(pl.multiple_of(head * ROWS, 256), ROWS)

    def kv_copy(h):
        return remote(kv_s.at[h], r0.at[:, mine, :], head_ss.at[h], head_rs.at[head], (blk, h))

    def kv_arrival(h):
        there = pl.ds(pl.multiple_of(h * PART, 32), PART)
        return remote(kv_s.at[h], r0.at[:, there, :], head_ss.at[h], head_rs.at[h], (blk, h))

    def q_copy(h):
        return remote(q_s.at[h], qh.at[rows_mine, :], q_ss.at[h], q_rs.at[head], (blk, h))

    def g_copy(h):
        return remote(g_s.at[h], gh.at[rows_mine, :], g_ss.at[h], g_rs.at[head], (blk, h))

    def q_arrival(h):
        there = pl.ds(pl.multiple_of(h * ROWS, 256), ROWS)
        return remote(q_s.at[h], qh.at[there, :], q_ss.at[h], q_rs.at[h], (blk, h))

    def g_arrival(h):
        there = pl.ds(pl.multiple_of(h * ROWS, 256), ROWS)
        return remote(g_s.at[h], gh.at[there, :], g_ss.at[h], g_rs.at[h], (blk, h))

    own_kv = pltpu.make_async_copy(kv_s.at[head], r0.at[:, mine, :], loc.at[0])
    own_q = pltpu.make_async_copy(q_s.at[head], qh.at[rows_mine, :], loc.at[1])
    own_g = pltpu.make_async_copy(g_s.at[head], gh.at[rows_mine, :], loc.at[2])
    own_kv.start()

    def send_kv(k, c):
        kv_copy(peer(k)).start()
        return c

    def send_q(k, c):
        q_copy(peer(k)).start()
        return c

    def send_g(k, c):
        g_copy(peer(k)).start()
        return c

    lax.fori_loop(1, NH, send_kv, 0)
    zero = jnp.zeros((BS, DH), F32)
    for ref in (awk, awv, agk, agv, ark, arv):
        def clear(n, c, ref=ref):
            ref[pl.ds(pl.multiple_of(n * BS, BS), BS), :] = zero
            return c
        lax.fori_loop(0, ref.shape[0] // BS, clear, 0)

    own_kv.wait()

    def wait_kv(k, c):
        kv_arrival((head + k) % NH).wait_recv()
        return c

    lax.fori_loop(1, NH, wait_kv, 0)

    plus = [r0, rp1, rp2, rp3, r4]
    minus = [r0, rm1, rm2, rm3, r4]

    def z_copy(step, half, upward):
        chain = plus if upward else minus
        ss, rs = (zp_ss, zp_rs) if upward else (zm_ss, zm_rs)
        return remote(
            chain[step].at[half], chain[step + 1].at[half],
            ss.at[step, half], rs.at[step, half], up if upward else down,
        )

    to_after = remote(r0.at[:, pl.ds(ROWS - BS, BS), :], edge.at[0], e_ss.at[0], e_rs.at[0], after)
    to_before = remote(r0.at[:, pl.ds(0, BS), :], edge.at[1], e_ss.at[1], e_rs.at[1], before)
    for half in (0, 1):
        z_copy(0, half, True).start()
        z_copy(0, half, False).start()
    to_after.start()
    to_before.start()
    own_q.start()
    own_g.start()
    lax.fori_loop(1, NH, send_q, 0)
    lax.fori_loop(1, NH, send_g, 0)

    glob = [tab[T_GLOB + j] for j in range(2)]
    g_within = [tab[T_GLOB + 2 + j] for j in range(2)]

    def ar_y(n, dy):
        return remote(ga.at[n, (y + dy) % NY], gy.at[n, y], a0_ss.at[n, dy], a0_rs.at[n, NY - dy], column(dy))

    def ar_z(n, dz):
        rows = pl.ds(pl.multiple_of(((z + dz) % NZ) * PIECE, PIECE), PIECE)
        return remote(gp.at[n, rows, :], gz.at[n, z], a1_ss.at[n, dz], a1_rs.at[n, NZ - dz], ring(dz))

    z_rows = pl.ds(pl.multiple_of(z * PIECE, PIECE), PIECE)

    def ar_zback(n, dz):
        return remote(gm.at[n], gf.at[n, z_rows, :], a2_ss.at[n, dz], a2_rs.at[n, NZ - dz], ring(dz))

    def ar_yback(n, dy):
        return remote(gf.at[n], gall.at[n, y], a3_ss.at[n, dy], a3_rs.at[n, NY - dy], column(dy))

    def each(count, make, what):
        def one(d, c):
            copy = make(d)
            copy.start() if what == "start" else copy.wait_send()
            return c
        lax.fori_loop(1, count, one, 0)

    def ar_start(n):
        each(NY, functools.partial(ar_y, n), "start")
        gy[n, y] = ga[n, y]

    def ar_one(n):
        for dy in range(1, NY):
            remote(ga.at[n, y], gy.at[n, (y + dy) % NY], a0_ss.at[n, dy], a0_rs.at[n, dy], column(dy)).wait_recv()
        total = gy[n, 0].astype(F32)
        for k in range(1, NY):
            total += gy[n, k].astype(F32)
        gp[n] = total.astype(BF16)
        each(NZ, functools.partial(ar_z, n), "start")
        gz[n, z] = gp[n, z_rows, :]

    def ar_two(n):
        for dz in range(1, NZ):
            remote(gm.at[n], gz.at[n, (z + dz) % NZ], a1_ss.at[n, dz], a1_rs.at[n, dz], ring(dz)).wait_recv()
        total = gz[n, 0].astype(F32)
        for k in range(1, NZ):
            total += gz[n, k].astype(F32)
        gm[n] = total.astype(BF16)
        each(NZ, functools.partial(ar_zback, n), "start")
        gf[n, z_rows, :] = gm[n]

    def ar_three(n):
        for dz in range(1, NZ):
            rows = pl.ds(pl.multiple_of(((z + dz) % NZ) * PIECE, PIECE), PIECE)
            remote(gm.at[n], gf.at[n, rows, :], a2_ss.at[n, dz], a2_rs.at[n, dz], ring(dz)).wait_recv()
        each(NY, functools.partial(ar_yback, n), "start")
        gall[n, y] = gf[n]

    def ar_end(n):
        for dy in range(1, NY):
            remote(gf.at[n], gall.at[n, (y + dy) % NY], a3_ss.at[n, dy], a3_rs.at[n, dy], column(dy)).wait_recv()

    def ar_drain(n):
        each(NY, functools.partial(ar_y, n), "wait")
        each(NZ, functools.partial(ar_z, n), "wait")
        each(NZ, functools.partial(ar_zback, n), "wait")
        each(NY, functools.partial(ar_yback, n), "wait")

    def block_rows(w):
        return pl.ds(w * BS, BS)

    def y_copy(dy, index, shard_z):
        dev = column(dy)
        return remote(
            xs.at[index * 4 + dy], xr.at[y * NZ + shard_z],
            y_ss.at[index, dy], y_rs.at[index, (NY - dy) % NY], dev,
        )

    def y_arrival(dy, index, shard_z):
        return remote(
            xs.at[index * 4 + dy], xr.at[((y + dy) % NY) * NZ + shard_z],
            y_ss.at[index, dy], y_rs.at[index, dy], column(dy),
        )

    order = [(r0, 0), (rp1, -1), (rm1, 1), (rp2, -2), (rm2, 2), (rp3, -3), (rm3, 3), (r4, 4)]

    def shard_of(delta):
        return (z + delta + NZ) % NZ

    def serve(index):
        buf, delta = order[index]
        sz = shard_of(delta)

        def one(dy, c):
            w = tab[T_PICK + ((y + dy) % NY) * NZ + sz]
            xs[index * 4 + dy] = buf[:, block_rows(w), :]
            y_copy(dy, index, sz).start()
            return c

        lax.fori_loop(1, NY, one, 0)
        w = tab[T_PICK + y * NZ + sz]
        xr[y * NZ + sz] = buf[:, block_rows(w), :]
    def place(i, s, kb, vb):
        if s < 5:
            k_list, v_list, kt_list, vt_list, at = lkn, lvn, lktn, lvtn, s * BS
        else:
            k_list, v_list, kt_list, vt_list, at = lkf, lvf, lktf, lvtf, (s - 5) * BS
        k_list[i, at:at + BS, :] = kb
        v_list[i, at:at + BS, :] = vb
        kt_list[i, :, at:at + BS] = turned(kb)
        vt_list[i, :, at:at + BS] = turned(vb)

    def turned(block):
        return block.astype(F32).T.astype(BF16)

    def place_window(e, kb, vb):
        for s in range(3):
            if 0 <= e - s < QB:
                place(e - s, s, kb, vb)

    def chunks_of(h):
        js = [h * 3 + t for t in range(3)]
        return js, [j // 4 for j in js], [pl.ds(pl.multiple_of(j * CHUNK, CHUNK), CHUNK) for j in js]

    turns = range(3)
    nt, nn = ((1,), (1,)), ((1,), (0,))

    def attend_near(h):
        js, at, rows = chunks_of(h)
        st = [dot(lkn[at[t]], qh[rows[t], :], nt) for t in turns]
        peak = [jnp.max(v, axis=0, keepdims=True) for v in st]
        ex = [jnp.exp2((st[t] - peak[t]) * (SCALE * LOG2E)) for t in turns]
        total = [jnp.sum(v, axis=0, keepdims=True) for v in ex]
        eb = [v.astype(BF16) for v in ex]
        ot = [dot(lvtn[at[t]], eb[t], nn) for t in turns]
        for t in turns:
            exn[js[t]] = eb[t]
            o1[js[t]] = ot[t]
            stats[js[t], 0:1, :] = peak[t]
            stats[js[t], 1:2, :] = total[t]

    def attend_far(h):
        js, at, rows = chunks_of(h)
        q = [qh[r, :] for r in rows]
        g = [gh[r, :] for r in rows]
        first = [stats[j, 0:1, :] for j in js]
        first_total = [stats[j, 1:2, :] for j in js]
        first_out = [o1[j] for j in js]
        st = [dot(lkf[at[t]], q[t], nt) for t in turns]
        dpt = [dot(lvf[at[t]], g[t], nt) for t in turns]
        gt = [v.astype(F32).T for v in g]
        peak = [jnp.maximum(first[t], jnp.max(st[t], axis=0, keepdims=True)) for t in turns]
        shrink = [jnp.exp2((first[t] - peak[t]) * (SCALE * LOG2E)) for t in turns]
        ex = [jnp.exp2((st[t] - peak[t]) * (SCALE * LOG2E)) for t in turns]
        inv = [1.0 / (shrink[t] * first_total[t] + jnp.sum(ex[t], axis=0, keepdims=True)) for t in turns]
        near = [shrink[t] * inv[t] for t in turns]
        pt = [ex[t] * inv[t] for t in turns]
        pb = [v.astype(BF16) for v in pt]
        ot = [first_out[t] * near[t] + dot(lvtf[at[t]], pb[t], nn) for t in turns]
        delta = [jnp.sum(ot[t].astype(BF16).astype(F32) * gt[t], axis=0, keepdims=True) for t in turns]
        ds = [(pt[t] * (dpt[t] - delta[t])).astype(BF16) for t in turns]
        dv = [dot(pb[t], g[t], nn) for t in turns]
        dk = [dot(ds[t], q[t], nn) for t in turns]
        for t in turns:
            ob[rows[t], :] = ot[t].T.astype(BF16)
            stats[js[t], 2:3, :] = near[t]
            stats[js[t], 3:4, :] = delta[t]
            dsf[js[t]] = ds[t]
        for t in turns:
            rbase = pl.ds(pl.multiple_of(at[t] * FAR, BS), FAR)
            arv[rbase, :] += dv[t]
            ark[rbase, :] += dk[t]

    def attend_back(h):
        js, at, rows = chunks_of(h)
        q = [qh[r, :] for r in rows]
        g = [gh[r, :] for r in rows]
        dpt = [dot(lvn[at[t]], g[t], nt) for t in turns]
        pt = [exn[js[t]].astype(F32) * stats[js[t], 2:3, :] for t in turns]
        pb = [v.astype(BF16) for v in pt]
        ds = [(pt[t] * (dpt[t] - stats[js[t], 3:4, :])).astype(BF16) for t in turns]
        dqt = [dot(lktn[at[t]], ds[t], nn) + dot(lktf[at[t]], dsf[js[t]], nn) for t in turns]
        dv = [dot(pb[t], g[t], nn) for t in turns]
        dk = [dot(ds[t], q[t], nn) for t in turns]
        for t in turns:
            dqb[rows[t], :] = (dqt[t] * SCALE).T.astype(BF16)
        for t in turns:
            base = pl.ds(pl.multiple_of(at[t] * BS, BS), 3 * BS)
            awk[base, :] += dk[t][0:3 * BS]
            awv[base, :] += dv[t][0:3 * BS]
        agk[...] += dk[0][3 * BS:] + dk[1][3 * BS:] + dk[2][3 * BS:]
        agv[...] += dv[0][3 * BS:] + dv[1][3 * BS:] + dv[2][3 * BS:]

    def near_parts(first, last):
        def part(k, c):
            h = peer(k)

            @pl.when(k > 0)
            def _():
                q_arrival(h).wait_recv()

            attend_near(h)
            return c

        lax.fori_loop(first, last, part, 0)

    for j in range(2):
        here = flag(tab[T_GLOB + 4 + j], blk)
        for half in range(2):
            picked = r0[half, block_rows(g_within[j]), :].astype(F32)
            ga[0, 2 * j + half] = (picked * here).astype(BF16)
    ar_start(0)
    serve(0)
    for e in range(1, QB + 1):
        place_window(e, r0[0, (e - 1) * BS:e * BS, :], r0[1, (e - 1) * BS:e * BS, :])
    ar_one(0)

    def forward(step, half):
        z_copy(step - 1, half, True).wait_recv()
        if step < 3 or half == 0:
            z_copy(step, half, True).start()
        z_copy(step - 1, half, False).wait_recv()
        if step < 3 or half == 1:
            z_copy(step, half, False).start()

    forward(1, 0)
    ar_two(0)
    to_after.wait_recv()
    to_before.wait_recv()
    place_window(0, edge[0, 0], edge[0, 1])
    place_window(QB + 1, edge[1, 0], edge[1, 1])
    forward(1, 1)
    serve(1)
    serve(2)
    ar_three(0)
    forward(2, 0)
    ar_end(0)
    for j in range(2):
        for i in range(QB):
            place(i, 3 + j, gall[0, 2 * j], gall[0, 2 * j + 1])
    forward(2, 1)
    serve(3)
    serve(4)
    own_q.wait()
    near_parts(0, 2)
    forward(3, 0)
    near_parts(2, 4)
    forward(3, 1)
    serve(5)
    serve(6)
    near_parts(4, 6)
    z_copy(3, 0, True).wait_recv()
    z_copy(3, 1, False).wait_recv()
    serve(7)
    near_parts(6, 8)

    for index in range(8):
        def wait_y(dy, c, index=index):
            y_arrival(dy, index, shard_of(order[index][1])).wait_recv()
            return c
        lax.fori_loop(1, NY, wait_y, 0)

    def place_random(i, c):
        for r in range(RAND):
            owner = tab[T_OWN + i * RAND + r]
            place(i, 5 + r, xr[owner, 0], xr[owner, 1])
        return c

    lax.fori_loop(0, QB, place_random, 0)
    own_g.wait()

    def wait_g(k, c):
        g_arrival(peer(k)).wait_recv()
        return c

    lax.fori_loop(1, NH, wait_g, 0)

    def there_rows(h):
        return pl.ds(pl.multiple_of(h * ROWS, 256), ROWS)

    def o_copy(h):
        return remote(ob.at[there_rows(h), :], o_out.at[head], o_ss.at[h], o_rs.at[head], (blk, h))

    def dq_copy(h):
        return remote(dqb.at[there_rows(h), :], dq_out.at[head], dq_ss.at[h], dq_rs.at[head], (blk, h))

    def o_arrival(h):
        return remote(ob.at[there_rows(h), :], o_out.at[h], o_ss.at[h], o_rs.at[h], (blk, h))

    def dq_arrival(h):
        return remote(dqb.at[there_rows(h), :], dq_out.at[h], dq_ss.at[h], dq_rs.at[h], (blk, h))

    own_o = pltpu.make_async_copy(ob.at[there_rows(head), :], o_out.at[head], loc.at[3])
    own_dq = pltpu.make_async_copy(dqb.at[there_rows(head), :], dq_out.at[head], loc.at[4])

    def far_part(n, c):
        k = NH - 1 - n
        h = peer(k)
        attend_far(h)

        @pl.when(k > 0)
        def _():
            o_copy(h).start()

        return c

    lax.fori_loop(0, NH, far_part, 0)
    own_o.start()

    def back_parts(first, last):
        def part(n, c):
            k = NH - 1 - n
            h = peer(k)
            attend_back(h)

            @pl.when(k > 0)
            def _():
                dq_copy(h).start()

            return c

        lax.fori_loop(first, last, part, 0)

    def w_copy(dy, index):
        return remote(
            ys.at[index * 4 + dy], yr.at[index * 4 + y],
            w_ss.at[index, dy], w_rs.at[index, (NY - dy) % NY], column(dy),
        )

    def w_arrival(dy, index):
        return remote(
            ys.at[index * 4 + dy], yr.at[index * 4 + (y + dy) % NY],
            w_ss.at[index, dy], w_rs.at[index, dy], column(dy),
        )

    back = [4, 3, -3, 2, -2, 1, -1, 0]

    def slot_rows(slot):
        return pl.ds(slot * BS, BS)

    def give(index):
        sz = shard_of(back[index])

        def one(dy, c):
            slot = tab[T_SLOT + ((y + dy) % NY) * NZ + sz]
            ys[index * 4 + dy, 0] = (ark[slot_rows(slot), :] * SCALE).astype(BF16)
            ys[index * 4 + dy, 1] = arv[slot_rows(slot), :].astype(BF16)
            w_copy(dy, index).start()
            return c

        lax.fori_loop(1, NY, one, 0)
        slot = tab[T_SLOT + y * NZ + sz]
        yr[index * 4 + y, 0] = (ark[slot_rows(slot), :] * SCALE).astype(BF16)
        yr[index * 4 + y, 1] = arv[slot_rows(slot), :].astype(BF16)

    def add_up(index, part):
        sz = shard_of(back[index])

        def wait_w(dy, c):
            w_arrival(dy, index).wait_recv()
            return c

        lax.fori_loop(1, NY, wait_w, 0)
        hits = [tab[T_WANT + yy * NZ + sz] for yy in range(NY)]

        def one_block(b, c):
            for half in range(2):
                total = yr[index * 4, half].astype(part.dtype) * flag(hits[0], b).astype(part.dtype)
                for yy in range(1, NY):
                    total += yr[index * 4 + yy, half].astype(part.dtype) * flag(hits[yy], b).astype(part.dtype)
                part[half, pl.ds(pl.multiple_of(b * BS, BS), BS), :] = total
            return c

        lax.fori_loop(0, QB, one_block, 0)

    def p_copy(step, half, upward):
        if upward:
            return remote(ssp.at[step, half], srp.at[step, half], pp_ss.at[step, half], pp_rs.at[step, half], up)
        return remote(ssm.at[step, half], srm.at[step, half], pm_ss.at[step, half], pm_rs.at[step, half], down)

    def pass_on(step):
        for waits in (False, True):
            for upward in (True, False):
                send, recv, part = (ssp, srp, partp) if upward else (ssm, srm, partm)
                first = 0 if upward else 1
                for half in (first, 1 - first):
                    if waits != (step > 1 or half == first):
                        continue
                    total = part[half].astype(F32)
                    if waits:
                        p_copy(step - 1, half, upward).wait_recv()
                        total += recv[step - 1, half].astype(F32)
                    send[step, half] = total.astype(BF16)
                    p_copy(step, half, upward).start()

    give(0)
    give(1)
    give(2)
    back_parts(0, 2)
    add_up(0, partp)
    ssp[0, 0] = partp[0].astype(BF16)
    p_copy(0, 0, True).start()
    ssm[0, 1] = partp[1].astype(BF16)
    p_copy(0, 1, False).start()
    give(3)
    give(4)
    add_up(1, partp)
    add_up(2, partm)
    back_parts(2, 4)
    pass_on(1)
    give(5)
    give(6)
    add_up(3, partp)
    add_up(4, partm)
    back_parts(4, 8)
    own_dq.start()
    for n, at in ((0, 0), (1, QB + 1)):
        rows = slice(at * BS, (at + 1) * BS)
        es[n, 0] = (awk[rows, :] * SCALE).astype(BF16)
        es[n, 1] = awv[rows, :].astype(BF16)
    e2_before = remote(es.at[0], er.at[1], e2_ss.at[0], e2_rs.at[1], before)
    e2_after = remote(es.at[1], er.at[0], e2_ss.at[1], e2_rs.at[0], after)
    e2_before.start()
    e2_after.start()
    for j in range(2):
        rows = slice(j * BS, (j + 1) * BS)
        ga[1, 2 * j] = (agk[rows, :] * SCALE).astype(BF16)
        ga[1, 2 * j + 1] = agv[rows, :].astype(BF16)
    ar_start(1)
    pass_on(2)
    give(7)
    ar_one(1)
    add_up(5, partp)
    add_up(6, partm)
    pass_on(3)
    ar_two(1)
    add_up(7, fin)
    e2_before.wait_send()
    e2_after.wait_send()
    remote(es.at[0], er.at[1], e2_ss.at[0], e2_rs.at[1], before).wait_recv()
    remote(es.at[1], er.at[0], e2_ss.at[1], e2_rs.at[0], after).wait_recv()
    for half, window in ((0, awk), (1, awv)):
        factor = SCALE if half == 0 else 1.0
        for b in range(QB):
            rows = slice(b * BS, (b + 1) * BS)
            total = window[(b + 1) * BS:(b + 2) * BS, :] * factor + fin[half, rows, :]
            if b == 0:
                total += er[0, half].astype(F32)
            if b == QB - 1:
                total += er[1, half].astype(F32)
            fin[half, rows, :] = total
    ar_three(1)
    ar_end(1)
    for half in range(2):
        p_copy(3, half, True).wait_recv()
        p_copy(3, half, False).wait_recv()
        for b in range(QB):
            rows = slice(b * BS, (b + 1) * BS)
            total = fin[half, rows, :]
            total += srp[3, half, rows, :].astype(F32) + srm[3, half, rows, :].astype(F32)
            for j in range(2):
                total += gall[1, 2 * j + half].astype(F32) * flag(glob[j], blk * QB + b)
            dkvb[half, rows, :] = total.astype(BF16)

    def part_rows(h):
        return pl.ds(pl.multiple_of(h * PART, 32), PART)

    def dkv_copy(h):
        return remote(dkvb.at[:, part_rows(h), :], dkv_out.at[head], dkv_ss.at[h], dkv_rs.at[head], (blk, h))

    def dkv_arrival(h):
        return remote(dkvb.at[:, part_rows(h), :], dkv_out.at[h], dkv_ss.at[h], dkv_rs.at[h], (blk, h))

    own_dkv = pltpu.make_async_copy(dkvb.at[:, mine, :], dkv_out.at[head], loc.at[5])

    def send_dkv(k, c):
        dkv_copy(peer(k)).start()
        return c

    lax.fori_loop(1, NH, send_dkv, 0)
    own_dkv.start()

    def drain(k, c):
        h = (head + k) % NH
        kv_copy(h).wait_send()
        q_copy(h).wait_send()
        g_copy(h).wait_send()
        o_copy(h).wait_send()
        dq_copy(h).wait_send()
        dkv_copy(h).wait_send()
        o_arrival(h).wait_recv()
        dq_arrival(h).wait_recv()
        dkv_arrival(h).wait_recv()
        return c

    for step in range(4):
        for half in range(2):
            if step < 3 or half == 0:
                z_copy(step, half, True).wait_send()
            if step < 3 or half == 1:
                z_copy(step, half, False).wait_send()
            if step > 0 or half == 0:
                p_copy(step, half, True).wait_send()
            if step > 0 or half == 1:
                p_copy(step, half, False).wait_send()
    to_after.wait_send()
    to_before.wait_send()

    def drain_column(dy, c):
        for index in range(8):
            y_copy(dy, index, shard_of(order[index][1])).wait_send()
            w_copy(dy, index).wait_send()
        return c

    lax.fori_loop(1, NY, drain_column, 0)
    ar_drain(0)
    ar_drain(1)
    lax.fori_loop(1, NH, drain, 0)
    own_o.wait()
    own_dq.wait()
    own_dkv.wait()


def tables(rand_blocks, global_blocks):
    blk = lax.axis_index("blk")
    head = lax.axis_index("head")
    y, z = blk // NZ, blk % NZ
    chosen = lax.dynamic_slice_in_dim(rand_blocks, head, 1, 1).reshape(NY, NZ, SLOTS)
    column = lax.dynamic_slice_in_dim(chosen, z, 1, 1)
    owners = y * NZ + jnp.arange(NZ, dtype=jnp.int32)[None, :, None]
    want = jnp.max(jnp.where(column // QB == owners, column % QB, -1), axis=2)
    own = lax.dynamic_slice_in_dim(chosen.reshape(NY * NZ, SLOTS), blk, 1, 0)[0] // QB
    shards = jnp.arange(NY * NZ, dtype=jnp.int32)[:, None]
    slot = jnp.max(
        jnp.where(own[None, :] == shards, jnp.arange(SLOTS, dtype=jnp.int32)[None, :], 0), axis=1
    )
    want = want.reshape(-1)
    picked = jnp.maximum(want, 0)
    shard = global_blocks // QB
    return jnp.concatenate(
        [want, picked, own, slot, global_blocks, global_blocks % QB, shard]
    )


def on_device(queries, keys, values, out_grad, rand_blocks, global_blocks):
    tab = tables(rand_blocks, global_blocks)
    heads = queries.shape[1] // NH
    q_s = queries.reshape(PART, NH, heads, DH).transpose(1, 0, 2, 3).reshape(NH, ROWS, DH)
    g_s = out_grad.reshape(PART, NH, heads, DH).transpose(1, 0, 2, 3).reshape(NH, ROWS, DH)
    kv_s = jnp.stack([keys, values]).transpose(2, 0, 1, 3)
    vm = lambda shape, dtype=BF16: pltpu.VMEM(shape, dtype)
    dma = lambda *shape: pltpu.SemaphoreType.DMA(shape)
    total = NH * ROWS
    pair = (2, BS, DH)
    anywhere = pl.BlockSpec(memory_space=pl.ANY)
    o_h, dq_h, dkv_h = pl.pallas_call(
        body,
        out_shape=(
            jax.ShapeDtypeStruct((NH, ROWS, DH), BF16),
            jax.ShapeDtypeStruct((NH, ROWS, DH), BF16),
            jax.ShapeDtypeStruct((NH, 2, PART, DH), BF16),
        ),
        in_specs=[pl.BlockSpec(memory_space=pltpu.SMEM), anywhere, anywhere, anywhere],
        out_specs=(anywhere, anywhere, anywhere),
        scratch_shapes=[
            vm((total, DH)), vm((total, DH)),
            *[vm((2, ROWS, DH)) for _ in range(8)],
            vm((32,) + pair), vm((32,) + pair), vm((2,) + pair),
            vm((QB, NEAR, DH)), vm((QB, NEAR, DH)), vm((QB, DH, NEAR)), vm((QB, DH, NEAR)),
            vm((QB, FAR, DH)), vm((QB, FAR, DH)), vm((QB, DH, FAR)), vm((QB, DH, FAR)),
            vm((CHUNKS, NEAR, CHUNK)), vm((CHUNKS, FAR, CHUNK)), vm((CHUNKS, DH, CHUNK), F32),
            vm((CHUNKS, 8, CHUNK), F32),
            vm((total, DH)), vm((total, DH)),
            vm(((QB + 2) * BS, DH), F32), vm(((QB + 2) * BS, DH), F32),
            vm((2 * BS, DH), F32), vm((2 * BS, DH), F32),
            vm((SLOTS * BS, DH), F32), vm((SLOTS * BS, DH), F32),
            vm((32,) + pair), vm((32,) + pair), vm((2,) + pair), vm((2,) + pair),
            vm((2, ROWS, DH)), vm((2, ROWS, DH)), vm((2, ROWS, DH), F32),
            *[vm((4, 2, ROWS, DH)) for _ in range(4)],
            vm((2, ROWS, DH)),
            vm((2, NY, BS, DH)), vm((2, NY, BS, DH)), vm((2, BS, DH)), vm((2, NZ, PIECE, DH)),
            vm((2, PIECE, DH)), vm((2, BS, DH)), vm((2, NY, BS, DH)),
            dma(NH), dma(NH), dma(NH), dma(NH), dma(NH), dma(NH), dma(6),
            dma(4, 2), dma(4, 2), dma(4, 2), dma(4, 2), dma(2), dma(2), dma(8, NY), dma(8, NY),
            dma(2, NY), dma(2, NY), dma(2, NZ), dma(2, NZ), dma(2, NZ), dma(2, NZ), dma(2, NY), dma(2, NY),
            dma(NH), dma(NH), dma(NH), dma(NH), dma(8, NY), dma(8, NY), dma(2), dma(2),
            dma(4, 2), dma(4, 2), dma(4, 2), dma(4, 2), dma(NH), dma(NH),
        ],
        compiler_params=pltpu.CompilerParams(
            collective_id=0, has_side_effects=True, vmem_limit_bytes=60 * 2**20
        ),
    )(tab, q_s, g_s, kv_s)

    def rows_back(part):
        return part.reshape(NH, PART, heads, DH).transpose(1, 0, 2, 3).reshape(PART, NH * heads, DH)

    kv_back = dkv_h.transpose(1, 2, 0, 3)
    return rows_back(o_h), rows_back(dq_h), kv_back[0], kv_back[1]


def solution(mesh):
    rows = P(("blk", "head"), None, None)
    return jax.shard_map(
        on_device,
        mesh=mesh,
        in_specs=(rows, rows, rows, rows, P(), P()),
        out_specs=(rows, rows, rows, rows),
        check_vma=False,
    )
```

```python
import functools
import math

import jax
import jax.numpy as jnp
from jax import lax
from jax.experimental import pallas as pl
from jax.experimental.pallas import tpu as pltpu
from jax.sharding import PartitionSpec as P

MESH = pl.DeviceIdType.MESH
NY, NZ, NH = 4, 8, 8
QB, BS, DH, RAND = 6, 128, 128, 3
ROWS = QB * BS
PART = ROWS // NH
LIST = 8 * BS
CHUNK = 256
NEAR, FAR = 5 * BS, RAND * BS
CHUNKS = NH * ROWS // CHUNK
PIECE = BS // NZ
SLOTS = QB * RAND
SCALE = 1.0 / math.sqrt(DH)
LOG2E = 1.4426950408889634
F32, BF16 = jnp.float32, jnp.bfloat16

T_WANT, T_PICK, T_OWN, T_SLOT, T_GLOB = 0, 32, 64, 82, 114


def dot(a, b, dims):
    return lax.dot_general(a, b, (dims, ((), ())), preferred_element_type=F32)


def flag(a, b):
    return (a == b).astype(jnp.int32).astype(F32)


def body(
    tab, q_in, g_in, kv_s, o_out, dq_out, dkv_out,
    qh, gh, r0, rp1, rp2, rp3, rm1, rm2, rm3, r4, xs, xr, edge,
    lkn, lvn, lktn, lvtn, lkf, lvf, lktf, lvtf, exn, dsf, o1, stats, ob, dqb,
    awk, awv, agk, agv, ark, arv,
    ys, yr, es, er, partp, partm, fin, ssp, ssm, srp, srm, dkvb,
    ga, gy, gp, gz, gm, gf, gall, raw,
    head_ss, head_rs, q_ss, q_rs, g_ss, g_rs, loc,
    zp_ss, zp_rs, zm_ss, zm_rs, e_ss, e_rs, y_ss, y_rs,
    a0_ss, a0_rs, a1_ss, a1_rs, a2_ss, a2_rs, a3_ss, a3_rs,
    o_ss, o_rs, dq_ss, dq_rs, w_ss, w_rs, e2_ss, e2_rs,
    pp_ss, pp_rs, pm_ss, pm_rs, dkv_ss, dkv_rs,
):
    blk = lax.axis_index("blk")
    head = lax.axis_index("head")
    y, z = blk // NZ, blk % NZ
    x, core = head // 2, head % 2
    up = (y * NZ + (z + 1) % NZ, head)
    down = (y * NZ + (z + NZ - 1) % NZ, head)
    after = ((blk + 1) % (NY * NZ), head)
    before = ((blk + NY * NZ - 1) % (NY * NZ), head)

    def column(dy):
        return (((y + dy) % NY) * NZ + z, head)

    def ring(dz):
        return (y * NZ + (z + dz) % NZ, head)

    def peer(k):
        t = k // 2
        return ((x + t * (t + 1) // 2) % (NH // 2)) * 2 + (core + k) % 2

    def remote(src, dst, ss, rs, dev):
        return pltpu.make_async_remote_copy(
            src_ref=src, dst_ref=dst, send_sem=ss, recv_sem=rs, device_id=dev, device_id_type=MESH
        )

    raw_q = pltpu.make_async_copy(q_in, raw, loc.at[6])
    raw_g = pltpu.make_async_copy(g_in, raw, loc.at[7])
    raw_q.start()
    bar = pltpu.get_barrier_semaphore()

    def greet(dev):
        pl.semaphore_signal(bar, inc=1, device_id=dev, device_id_type=MESH)

    def greet_head(k, c):
        greet((blk, (head + k) % NH))
        return c

    lax.fori_loop(1, NH, greet_head, 0)
    for dev in (after, before):
        greet(dev)
    for dy in range(1, NY):
        greet(column(dy))

    def greet_ring(dz, c):
        greet(ring(dz))
        return c

    lax.fori_loop(1, NZ, greet_ring, 0)
    pl.semaphore_wait(bar, NH - 1 + 2 + NY - 1 + NZ - 1)

    mine = pl.ds(pl.multiple_of(head * PART, 32), PART)
    rows_mine = pl.ds(pl.multiple_of(head * ROWS, 256), ROWS)

    def there_rows(h):
        return pl.ds(pl.multiple_of(h * ROWS, 256), ROWS)

    def kv_copy(h, half):
        return remote(
            kv_s.at[h, half], r0.at[half, mine, :], head_ss.at[half, h], head_rs.at[half, head], (blk, h)
        )

    def kv_arrival(h, half):
        there = pl.ds(pl.multiple_of(h * PART, 32), PART)
        return remote(
            kv_s.at[h, half], r0.at[half, there, :], head_ss.at[half, h], head_rs.at[half, h], (blk, h)
        )

    def q_copy(h):
        return remote(ob.at[there_rows(h), :], qh.at[rows_mine, :], q_ss.at[h], q_rs.at[head], (blk, h))

    def g_copy(h):
        return remote(dqb.at[there_rows(h), :], gh.at[rows_mine, :], g_ss.at[h], g_rs.at[head], (blk, h))

    def q_arrival(h):
        there = pl.ds(pl.multiple_of(h * ROWS, 256), ROWS)
        return remote(ob.at[there_rows(h), :], qh.at[there, :], q_ss.at[h], q_rs.at[h], (blk, h))

    def g_arrival(h):
        there = pl.ds(pl.multiple_of(h * ROWS, 256), ROWS)
        return remote(dqb.at[there_rows(h), :], gh.at[there, :], g_ss.at[h], g_rs.at[h], (blk, h))

    own_kv = pltpu.make_async_copy(kv_s.at[head], r0.at[:, mine, :], loc.at[0])
    own_q = pltpu.make_async_copy(ob.at[rows_mine, :], qh.at[rows_mine, :], loc.at[1])
    own_g = pltpu.make_async_copy(dqb.at[rows_mine, :], gh.at[rows_mine, :], loc.at[2])
    own_kv.start()

    def send_k(k, c):
        kv_copy(peer(k), 0).start()
        return c

    def send_v(k, c):
        kv_copy(peer(k), 1).start()
        return c

    def send_q(k, c):
        q_copy(peer(k)).start()
        return c

    def send_g(k, c):
        g_copy(peer(k)).start()
        return c

    lax.fori_loop(1, NH, send_k, 0)
    lax.fori_loop(1, NH, send_v, 0)

    def regroup(dst):
        for h in range(NH):
            rows = raw[:, h * NH:(h + 1) * NH, :].astype(F32).reshape(ROWS, DH)
            dst[h * ROWS:(h + 1) * ROWS, :] = rows.astype(BF16)

    raw_q.wait()
    regroup(ob)
    raw_g.start()
    zero = jnp.zeros((BS, DH), F32)
    for ref in (awk, awv, agk, agv, ark, arv):
        def clear(n, c, ref=ref):
            ref[pl.ds(pl.multiple_of(n * BS, BS), BS), :] = zero
            return c
        lax.fori_loop(0, ref.shape[0] // BS, clear, 0)

    own_kv.wait()

    def wait_kv(half):
        def one(k, c):
            kv_arrival((head + k) % NH, half).wait_recv()
            return c
        lax.fori_loop(1, NH, one, 0)

    plus = [r0, rp1, rp2, rp3, r4]
    minus = [r0, rm1, rm2, rm3, r4]

    def z_copy(step, half, upward):
        chain = plus if upward else minus
        ss, rs = (zp_ss, zp_rs) if upward else (zm_ss, zm_rs)
        return remote(
            chain[step].at[half], chain[step + 1].at[half],
            ss.at[step, half], rs.at[step, half], up if upward else down,
        )

    to_after = remote(r0.at[:, pl.ds(ROWS - BS, BS), :], edge.at[0], e_ss.at[0], e_rs.at[0], after)
    to_before = remote(r0.at[:, pl.ds(0, BS), :], edge.at[1], e_ss.at[1], e_rs.at[1], before)
    for half in (0, 1):
        wait_kv(half)
        z_copy(0, half, True).start()
        z_copy(0, half, False).start()
        if half == 0:
            own_q.start()
            lax.fori_loop(1, NH, send_q, 0)
    to_after.start()
    to_before.start()

    glob = [tab[T_GLOB + j] for j in range(2)]
    g_within = [tab[T_GLOB + 2 + j] for j in range(2)]

    def ar_y(n, dy):
        return remote(ga.at[n, (y + dy) % NY], gy.at[n, y], a0_ss.at[n, dy], a0_rs.at[n, NY - dy], column(dy))

    def ar_z(n, dz):
        rows = pl.ds(pl.multiple_of(((z + dz) % NZ) * PIECE, PIECE), PIECE)
        return remote(gp.at[n, rows, :], gz.at[n, z], a1_ss.at[n, dz], a1_rs.at[n, NZ - dz], ring(dz))

    z_rows = pl.ds(pl.multiple_of(z * PIECE, PIECE), PIECE)

    def ar_zback(n, dz):
        return remote(gm.at[n], gf.at[n, z_rows, :], a2_ss.at[n, dz], a2_rs.at[n, NZ - dz], ring(dz))

    def ar_yback(n, dy):
        return remote(gf.at[n], gall.at[n, y], a3_ss.at[n, dy], a3_rs.at[n, NY - dy], column(dy))

    def each(count, make, what):
        def one(d, c):
            copy = make(d)
            copy.start() if what == "start" else copy.wait_send()
            return c
        lax.fori_loop(1, count, one, 0)

    def ar_start(n):
        each(NY, functools.partial(ar_y, n), "start")
        gy[n, y] = ga[n, y]

    def ar_one(n):
        for dy in range(1, NY):
            remote(ga.at[n, y], gy.at[n, (y + dy) % NY], a0_ss.at[n, dy], a0_rs.at[n, dy], column(dy)).wait_recv()
        total = gy[n, 0].astype(F32)
        for k in range(1, NY):
            total += gy[n, k].astype(F32)
        gp[n] = total.astype(BF16)
        each(NZ, functools.partial(ar_z, n), "start")
        gz[n, z] = gp[n, z_rows, :]

    def ar_two(n):
        for dz in range(1, NZ):
            remote(gm.at[n], gz.at[n, (z + dz) % NZ], a1_ss.at[n, dz], a1_rs.at[n, dz], ring(dz)).wait_recv()
        total = gz[n, 0].astype(F32)
        for k in range(1, NZ):
            total += gz[n, k].astype(F32)
        gm[n] = total.astype(BF16)
        each(NZ, functools.partial(ar_zback, n), "start")
        gf[n, z_rows, :] = gm[n]

    def ar_three(n):
        for dz in range(1, NZ):
            rows = pl.ds(pl.multiple_of(((z + dz) % NZ) * PIECE, PIECE), PIECE)
            remote(gm.at[n], gf.at[n, rows, :], a2_ss.at[n, dz], a2_rs.at[n, dz], ring(dz)).wait_recv()
        each(NY, functools.partial(ar_yback, n), "start")
        gall[n, y] = gf[n]

    def ar_end(n):
        for dy in range(1, NY):
            remote(gf.at[n], gall.at[n, (y + dy) % NY], a3_ss.at[n, dy], a3_rs.at[n, dy], column(dy)).wait_recv()

    def ar_drain(n):
        each(NY, functools.partial(ar_y, n), "wait")
        each(NZ, functools.partial(ar_z, n), "wait")
        each(NZ, functools.partial(ar_zback, n), "wait")
        each(NY, functools.partial(ar_yback, n), "wait")

    def block_rows(w):
        return pl.ds(w * BS, BS)

    def y_copy(dy, index, shard_z):
        dev = column(dy)
        return remote(
            xs.at[index * 4 + dy], xr.at[y * NZ + shard_z],
            y_ss.at[index, dy], y_rs.at[index, (NY - dy) % NY], dev,
        )

    def y_arrival(dy, index, shard_z):
        return remote(
            xs.at[index * 4 + dy], xr.at[((y + dy) % NY) * NZ + shard_z],
            y_ss.at[index, dy], y_rs.at[index, dy], column(dy),
        )

    order = [(r0, 0), (rp1, -1), (rm1, 1), (rp2, -2), (rm2, 2), (rp3, -3), (rm3, 3), (r4, 4)]

    def shard_of(delta):
        return (z + delta + NZ) % NZ

    def serve(index):
        buf, delta = order[index]
        sz = shard_of(delta)

        def one(dy, c):
            w = tab[T_PICK + ((y + dy) % NY) * NZ + sz]
            xs[index * 4 + dy] = buf[:, block_rows(w), :]
            y_copy(dy, index, sz).start()
            return c

        lax.fori_loop(1, NY, one, 0)
        w = tab[T_PICK + y * NZ + sz]
        xr[y * NZ + sz] = buf[:, block_rows(w), :]
    def place(i, s, kb, vb):
        if s < 5:
            k_list, v_list, kt_list, vt_list, at = lkn, lvn, lktn, lvtn, s * BS
        else:
            k_list, v_list, kt_list, vt_list, at = lkf, lvf, lktf, lvtf, (s - 5) * BS
        k_list[i, at:at + BS, :] = kb
        v_list[i, at:at + BS, :] = vb
        kt_list[i, :, at:at + BS] = turned(kb)
        vt_list[i, :, at:at + BS] = turned(vb)

    def turned(block):
        return block.astype(F32).T.astype(BF16)

    def place_window(e, kb, vb):
        for s in range(3):
            if 0 <= e - s < QB:
                place(e - s, s, kb, vb)

    def chunks_of(h):
        js = [h * 3 + t for t in range(3)]
        return js, [j // 4 for j in js], [pl.ds(pl.multiple_of(j * CHUNK, CHUNK), CHUNK) for j in js]

    turns = range(3)
    nt, nn = ((1,), (1,)), ((1,), (0,))

    def attend_near(h):
        js, at, rows = chunks_of(h)
        st = [dot(lkn[at[t]], qh[rows[t], :], nt) for t in turns]
        peak = [jnp.max(v, axis=0, keepdims=True) for v in st]
        ex = [jnp.exp2((st[t] - peak[t]) * (SCALE * LOG2E)) for t in turns]
        total = [jnp.sum(v, axis=0, keepdims=True) for v in ex]
        eb = [v.astype(BF16) for v in ex]
        ot = [dot(lvtn[at[t]], eb[t], nn) for t in turns]
        for t in turns:
            exn[js[t]] = eb[t]
            o1[js[t]] = ot[t]
            stats[js[t], 0:1, :] = peak[t]
            stats[js[t], 1:2, :] = total[t]

    def attend_far(h):
        js, at, rows = chunks_of(h)
        q = [qh[r, :] for r in rows]
        g = [gh[r, :] for r in rows]
        first = [stats[j, 0:1, :] for j in js]
        first_total = [stats[j, 1:2, :] for j in js]
        first_out = [o1[j] for j in js]
        st = [dot(lkf[at[t]], q[t], nt) for t in turns]
        dpt = [dot(lvf[at[t]], g[t], nt) for t in turns]
        gt = [v.astype(F32).T for v in g]
        peak = [jnp.maximum(first[t], jnp.max(st[t], axis=0, keepdims=True)) for t in turns]
        shrink = [jnp.exp2((first[t] - peak[t]) * (SCALE * LOG2E)) for t in turns]
        ex = [jnp.exp2((st[t] - peak[t]) * (SCALE * LOG2E)) for t in turns]
        inv = [1.0 / (shrink[t] * first_total[t] + jnp.sum(ex[t], axis=0, keepdims=True)) for t in turns]
        near = [shrink[t] * inv[t] for t in turns]
        pt = [ex[t] * inv[t] for t in turns]
        pb = [v.astype(BF16) for v in pt]
        ot = [first_out[t] * near[t] + dot(lvtf[at[t]], pb[t], nn) for t in turns]
        delta = [jnp.sum(ot[t].astype(BF16).astype(F32) * gt[t], axis=0, keepdims=True) for t in turns]
        ds = [(pt[t] * (dpt[t] - delta[t])).astype(BF16) for t in turns]
        dv = [dot(pb[t], g[t], nn) for t in turns]
        dk = [dot(ds[t], q[t], nn) for t in turns]
        for t in turns:
            ob[rows[t], :] = ot[t].T.astype(BF16)
            stats[js[t], 2:3, :] = near[t]
            stats[js[t], 3:4, :] = delta[t]
            dsf[js[t]] = ds[t]
        for t in turns:
            rbase = pl.ds(pl.multiple_of(at[t] * FAR, BS), FAR)
            arv[rbase, :] += dv[t]
            ark[rbase, :] += dk[t]

    def attend_back(h):
        js, at, rows = chunks_of(h)
        q = [qh[r, :] for r in rows]
        g = [gh[r, :] for r in rows]
        dpt = [dot(lvn[at[t]], g[t], nt) for t in turns]
        pt = [exn[js[t]].astype(F32) * stats[js[t], 2:3, :] for t in turns]
        pb = [v.astype(BF16) for v in pt]
        ds = [(pt[t] * (dpt[t] - stats[js[t], 3:4, :])).astype(BF16) for t in turns]
        dqt = [dot(lktn[at[t]], ds[t], nn) + dot(lktf[at[t]], dsf[js[t]], nn) for t in turns]
        dv = [dot(pb[t], g[t], nn) for t in turns]
        dk = [dot(ds[t], q[t], nn) for t in turns]
        for t in turns:
            dqb[rows[t], :] = (dqt[t] * SCALE).T.astype(BF16)
        for t in turns:
            base = pl.ds(pl.multiple_of(at[t] * BS, BS), 3 * BS)
            awk[base, :] += dk[t][0:3 * BS]
            awv[base, :] += dv[t][0:3 * BS]
        agk[...] += dk[0][3 * BS:] + dk[1][3 * BS:] + dk[2][3 * BS:]
        agv[...] += dv[0][3 * BS:] + dv[1][3 * BS:] + dv[2][3 * BS:]

    def near_parts(first, last):
        def part(k, c):
            h = peer(k)

            @pl.when(k > 0)
            def _():
                q_arrival(h).wait_recv()

            attend_near(h)
            return c

        lax.fori_loop(first, last, part, 0)

    for j in range(2):
        here = flag(tab[T_GLOB + 4 + j], blk)
        for half in range(2):
            picked = r0[half, block_rows(g_within[j]), :].astype(F32)
            ga[0, 2 * j + half] = (picked * here).astype(BF16)
    ar_start(0)
    serve(0)
    raw_g.wait()
    regroup(dqb)
    for e in range(1, QB + 1):
        place_window(e, r0[0, (e - 1) * BS:e * BS, :], r0[1, (e - 1) * BS:e * BS, :])
    ar_one(0)

    def forward(step, half):
        z_copy(step - 1, half, True).wait_recv()
        if step < 3 or half == 0:
            z_copy(step, half, True).start()
        z_copy(step - 1, half, False).wait_recv()
        if step < 3 or half == 1:
            z_copy(step, half, False).start()

    forward(1, 0)
    to_after.wait_recv()
    to_before.wait_recv()
    place_window(0, edge[0, 0], edge[0, 1])
    place_window(QB + 1, edge[1, 0], edge[1, 1])
    ar_two(0)
    forward(1, 1)
    own_g.start()
    lax.fori_loop(1, NH, send_g, 0)
    serve(1)
    serve(2)
    forward(2, 0)
    ar_three(0)
    forward(2, 1)
    serve(3)
    serve(4)
    ar_end(0)
    for j in range(2):
        for i in range(QB):
            place(i, 3 + j, gall[0, 2 * j], gall[0, 2 * j + 1])
    own_q.wait()
    forward(3, 0)
    near_parts(0, 2)
    forward(3, 1)
    serve(5)
    serve(6)
    near_parts(2, 4)
    z_copy(3, 0, True).wait_recv()
    z_copy(3, 1, False).wait_recv()
    serve(7)
    near_parts(4, 8)

    for index in range(8):
        def wait_y(dy, c, index=index):
            y_arrival(dy, index, shard_of(order[index][1])).wait_recv()
            return c
        lax.fori_loop(1, NY, wait_y, 0)

    def place_random(i, c):
        for r in range(RAND):
            owner = tab[T_OWN + i * RAND + r]
            place(i, 5 + r, xr[owner, 0], xr[owner, 1])
        return c

    lax.fori_loop(0, QB, place_random, 0)
    own_g.wait()

    def wait_g(k, c):
        g_arrival(peer(k)).wait_recv()
        return c

    lax.fori_loop(1, NH, wait_g, 0)

    def o_copy(h):
        return remote(ob.at[there_rows(h), :], o_out.at[head], o_ss.at[h], o_rs.at[head], (blk, h))

    def dq_copy(h):
        return remote(dqb.at[there_rows(h), :], dq_out.at[head], dq_ss.at[h], dq_rs.at[head], (blk, h))

    def o_arrival(h):
        return remote(ob.at[there_rows(h), :], o_out.at[h], o_ss.at[h], o_rs.at[h], (blk, h))

    def dq_arrival(h):
        return remote(dqb.at[there_rows(h), :], dq_out.at[h], dq_ss.at[h], dq_rs.at[h], (blk, h))

    own_o = pltpu.make_async_copy(ob.at[there_rows(head), :], o_out.at[head], loc.at[3])
    own_dq = pltpu.make_async_copy(dqb.at[there_rows(head), :], dq_out.at[head], loc.at[4])

    def far_part(n, c):
        k = NH - 1 - n
        h = peer(k)
        attend_far(h)

        @pl.when(k > 0)
        def _():
            o_copy(h).start()

        return c

    def staging_free(k, c):
        h = peer(k)
        q_copy(h).wait_send()
        g_copy(h).wait_send()
        return c

    lax.fori_loop(1, NH, staging_free, 0)
    lax.fori_loop(0, NH, far_part, 0)
    own_o.start()

    def back_parts(first, last):
        def part(n, c):
            k = NH - 1 - n
            h = peer(k)
            attend_back(h)

            @pl.when(k > 0)
            def _():
                dq_copy(h).start()

            return c

        lax.fori_loop(first, last, part, 0)

    def w_copy(dy, index):
        return remote(
            ys.at[index * 4 + dy], yr.at[index * 4 + y],
            w_ss.at[index, dy], w_rs.at[index, (NY - dy) % NY], column(dy),
        )

    def w_arrival(dy, index):
        return remote(
            ys.at[index * 4 + dy], yr.at[index * 4 + (y + dy) % NY],
            w_ss.at[index, dy], w_rs.at[index, dy], column(dy),
        )

    back = [4, 3, -3, 2, -2, 1, -1, 0]

    def slot_rows(slot):
        return pl.ds(slot * BS, BS)

    def give(index):
        sz = shard_of(back[index])

        def one(dy, c):
            slot = tab[T_SLOT + ((y + dy) % NY) * NZ + sz]
            ys[index * 4 + dy, 0] = (ark[slot_rows(slot), :] * SCALE).astype(BF16)
            ys[index * 4 + dy, 1] = arv[slot_rows(slot), :].astype(BF16)
            w_copy(dy, index).start()
            return c

        lax.fori_loop(1, NY, one, 0)
        slot = tab[T_SLOT + y * NZ + sz]
        yr[index * 4 + y, 0] = (ark[slot_rows(slot), :] * SCALE).astype(BF16)
        yr[index * 4 + y, 1] = arv[slot_rows(slot), :].astype(BF16)

    def add_up(index, part):
        sz = shard_of(back[index])

        def wait_w(dy, c):
            w_arrival(dy, index).wait_recv()
            return c

        lax.fori_loop(1, NY, wait_w, 0)
        hits = [tab[T_WANT + yy * NZ + sz] for yy in range(NY)]

        def one_block(b, c):
            for half in range(2):
                total = yr[index * 4, half].astype(part.dtype) * flag(hits[0], b).astype(part.dtype)
                for yy in range(1, NY):
                    total += yr[index * 4 + yy, half].astype(part.dtype) * flag(hits[yy], b).astype(part.dtype)
                part[half, pl.ds(pl.multiple_of(b * BS, BS), BS), :] = total
            return c

        lax.fori_loop(0, QB, one_block, 0)

    def p_copy(step, half, upward):
        if upward:
            return remote(ssp.at[step, half], srp.at[step, half], pp_ss.at[step, half], pp_rs.at[step, half], up)
        return remote(ssm.at[step, half], srm.at[step, half], pm_ss.at[step, half], pm_rs.at[step, half], down)

    def pass_on(step):
        for half in (0, 1):
            for upward in (half == 1, half == 0):
                send, recv, part = (ssp, srp, partp) if upward else (ssm, srm, partm)
                total = part[half].astype(F32)
                if step > 1 or half == (0 if upward else 1):
                    p_copy(step - 1, half, upward).wait_recv()
                    total += recv[step - 1, half].astype(F32)
                send[step, half] = total.astype(BF16)
                p_copy(step, half, upward).start()

    give(0)
    give(1)
    give(2)
    back_parts(0, 4)
    add_up(0, partp)
    ssp[0, 0] = partp[0].astype(BF16)
    p_copy(0, 0, True).start()
    ssm[0, 1] = partp[1].astype(BF16)
    p_copy(0, 1, False).start()
    give(3)
    give(4)
    add_up(1, partp)
    add_up(2, partm)
    back_parts(4, 8)
    own_dq.start()
    for n, at in ((0, 0), (1, QB + 1)):
        rows = slice(at * BS, (at + 1) * BS)
        es[n, 0] = (awk[rows, :] * SCALE).astype(BF16)
        es[n, 1] = awv[rows, :].astype(BF16)
    e2_before = remote(es.at[0], er.at[1], e2_ss.at[0], e2_rs.at[1], before)
    e2_after = remote(es.at[1], er.at[0], e2_ss.at[1], e2_rs.at[0], after)
    e2_before.start()
    e2_after.start()
    for j in range(2):
        rows = slice(j * BS, (j + 1) * BS)
        ga[1, 2 * j] = (agk[rows, :] * SCALE).astype(BF16)
        ga[1, 2 * j + 1] = agv[rows, :].astype(BF16)
    ar_start(1)
    pass_on(1)
    give(5)
    give(6)
    ar_one(1)
    add_up(3, partp)
    add_up(4, partm)
    pass_on(2)
    give(7)
    ar_two(1)
    add_up(5, partp)
    add_up(6, partm)
    pass_on(3)
    ar_three(1)
    add_up(7, fin)
    e2_before.wait_send()
    e2_after.wait_send()
    remote(es.at[0], er.at[1], e2_ss.at[0], e2_rs.at[1], before).wait_recv()
    remote(es.at[1], er.at[0], e2_ss.at[1], e2_rs.at[0], after).wait_recv()
    for half, window in ((0, awk), (1, awv)):
        factor = SCALE if half == 0 else 1.0
        for b in range(QB):
            rows = slice(b * BS, (b + 1) * BS)
            total = window[(b + 1) * BS:(b + 2) * BS, :] * factor + fin[half, rows, :]
            if b == 0:
                total += er[0, half].astype(F32)
            if b == QB - 1:
                total += er[1, half].astype(F32)
            fin[half, rows, :] = total
    def part_rows(h):
        return pl.ds(pl.multiple_of(h * PART, 32), PART)

    def dkv_copy(h, half):
        return remote(
            dkvb.at[half, part_rows(h), :], dkv_out.at[head, half],
            dkv_ss.at[half, h], dkv_rs.at[half, head], (blk, h),
        )

    def dkv_arrival(h, half):
        return remote(
            dkvb.at[half, part_rows(h), :], dkv_out.at[h, half],
            dkv_ss.at[half, h], dkv_rs.at[half, h], (blk, h),
        )

    def own_dkv(half):
        return pltpu.make_async_copy(dkvb.at[half, mine, :], dkv_out.at[head, half], loc.at[0 if half else 5])

    def send_dkv(half, k, c):
        dkv_copy(peer(k), half).start()
        return c

    ar_end(1)
    for half in range(2):
        p_copy(3, half, True).wait_recv()
        p_copy(3, half, False).wait_recv()
        for b in range(QB):
            rows = slice(b * BS, (b + 1) * BS)
            total = fin[half, rows, :]
            total += srp[3, half, rows, :].astype(F32) + srm[3, half, rows, :].astype(F32)
            for j in range(2):
                total += gall[1, 2 * j + half].astype(F32) * flag(glob[j], blk * QB + b)
            dkvb[half, rows, :] = total.astype(BF16)
        own_dkv(half).start()
        lax.fori_loop(1, NH, functools.partial(send_dkv, half), 0)

    def drain(k, c):
        h = (head + k) % NH
        kv_copy(h, 0).wait_send()
        kv_copy(h, 1).wait_send()
        o_copy(h).wait_send()
        dq_copy(h).wait_send()
        dkv_copy(h, 0).wait_send()
        dkv_copy(h, 1).wait_send()
        o_arrival(h).wait_recv()
        dq_arrival(h).wait_recv()
        dkv_arrival(h, 0).wait_recv()
        dkv_arrival(h, 1).wait_recv()
        return c

    for step in range(4):
        for half in range(2):
            if step < 3 or half == 0:
                z_copy(step, half, True).wait_send()
            if step < 3 or half == 1:
                z_copy(step, half, False).wait_send()
            if step > 0 or half == 0:
                p_copy(step, half, True).wait_send()
            if step > 0 or half == 1:
                p_copy(step, half, False).wait_send()
    to_after.wait_send()
    to_before.wait_send()

    def drain_column(dy, c):
        for index in range(8):
            y_copy(dy, index, shard_of(order[index][1])).wait_send()
            w_copy(dy, index).wait_send()
        return c

    lax.fori_loop(1, NY, drain_column, 0)
    ar_drain(0)
    ar_drain(1)
    lax.fori_loop(1, NH, drain, 0)
    own_o.wait()
    own_dq.wait()
    own_dkv(0).wait()
    own_dkv(1).wait()


def tables(rand_blocks, global_blocks):
    blk = lax.axis_index("blk")
    head = lax.axis_index("head")
    y, z = blk // NZ, blk % NZ
    chosen = lax.dynamic_slice_in_dim(rand_blocks, head, 1, 1).reshape(NY, NZ, SLOTS)
    column = lax.dynamic_slice_in_dim(chosen, z, 1, 1)
    owners = y * NZ + jnp.arange(NZ, dtype=jnp.int32)[None, :, None]
    want = jnp.max(jnp.where(column // QB == owners, column % QB, -1), axis=2)
    own = lax.dynamic_slice_in_dim(chosen.reshape(NY * NZ, SLOTS), blk, 1, 0)[0] // QB
    shards = jnp.arange(NY * NZ, dtype=jnp.int32)[:, None]
    slot = jnp.max(
        jnp.where(own[None, :] == shards, jnp.arange(SLOTS, dtype=jnp.int32)[None, :], 0), axis=1
    )
    want = want.reshape(-1)
    picked = jnp.maximum(want, 0)
    shard = global_blocks // QB
    return jnp.concatenate(
        [want, picked, own, slot, global_blocks, global_blocks % QB, shard]
    )


def on_device(queries, keys, values, out_grad, rand_blocks, global_blocks):
    tab = tables(rand_blocks, global_blocks)
    heads = queries.shape[1] // NH
    kv_s = jnp.stack([keys, values]).transpose(2, 0, 1, 3)
    vm = lambda shape, dtype=BF16: pltpu.VMEM(shape, dtype)
    dma = lambda *shape: pltpu.SemaphoreType.DMA(shape)
    total = NH * ROWS
    pair = (2, BS, DH)
    anywhere = pl.BlockSpec(memory_space=pl.ANY)
    o_h, dq_h, dkv_h = pl.pallas_call(
        body,
        out_shape=(
            jax.ShapeDtypeStruct((NH, ROWS, DH), BF16),
            jax.ShapeDtypeStruct((NH, ROWS, DH), BF16),
            jax.ShapeDtypeStruct((NH, 2, PART, DH), BF16),
        ),
        in_specs=[pl.BlockSpec(memory_space=pltpu.SMEM), anywhere, anywhere, anywhere],
        out_specs=(anywhere, anywhere, anywhere),
        scratch_shapes=[
            vm((total, DH)), vm((total, DH)),
            *[vm((2, ROWS, DH)) for _ in range(8)],
            vm((32,) + pair), vm((32,) + pair), vm((2,) + pair),
            vm((QB, NEAR, DH)), vm((QB, NEAR, DH)), vm((QB, DH, NEAR)), vm((QB, DH, NEAR)),
            vm((QB, FAR, DH)), vm((QB, FAR, DH)), vm((QB, DH, FAR)), vm((QB, DH, FAR)),
            vm((CHUNKS, NEAR, CHUNK)), vm((CHUNKS, FAR, CHUNK)), vm((CHUNKS, DH, CHUNK), F32),
            vm((CHUNKS, 8, CHUNK), F32),
            vm((total, DH)), vm((total, DH)),
            vm(((QB + 2) * BS, DH), F32), vm(((QB + 2) * BS, DH), F32),
            vm((2 * BS, DH), F32), vm((2 * BS, DH), F32),
            vm((SLOTS * BS, DH), F32), vm((SLOTS * BS, DH), F32),
            vm((32,) + pair), vm((32,) + pair), vm((2,) + pair), vm((2,) + pair),
            vm((2, ROWS, DH)), vm((2, ROWS, DH)), vm((2, ROWS, DH), F32),
            *[vm((4, 2, ROWS, DH)) for _ in range(4)],
            vm((2, ROWS, DH)),
            vm((2, NY, BS, DH)), vm((2, NY, BS, DH)), vm((2, BS, DH)), vm((2, NZ, PIECE, DH)),
            vm((2, PIECE, DH)), vm((2, BS, DH)), vm((2, NY, BS, DH)),
            vm(queries.shape),
            dma(2, NH), dma(2, NH), dma(NH), dma(NH), dma(NH), dma(NH), dma(8),
            dma(4, 2), dma(4, 2), dma(4, 2), dma(4, 2), dma(2), dma(2), dma(8, NY), dma(8, NY),
            dma(2, NY), dma(2, NY), dma(2, NZ), dma(2, NZ), dma(2, NZ), dma(2, NZ), dma(2, NY), dma(2, NY),
            dma(NH), dma(NH), dma(NH), dma(NH), dma(8, NY), dma(8, NY), dma(2), dma(2),
            dma(4, 2), dma(4, 2), dma(4, 2), dma(4, 2), dma(2, NH), dma(2, NH),
        ],
        compiler_params=pltpu.CompilerParams(
            collective_id=0, has_side_effects=True, vmem_limit_bytes=62 * 2**20
        ),
    )(tab, queries, out_grad, kv_s)

    def rows_back(part):
        return part.reshape(NH, PART, heads, DH).transpose(1, 0, 2, 3).reshape(PART, NH * heads, DH)

    kv_back = dkv_h.transpose(1, 2, 0, 3)
    return rows_back(o_h), rows_back(dq_h), kv_back[0], kv_back[1]


def solution(mesh):
    rows = P(("blk", "head"), None, None)
    return jax.shard_map(
        on_device,
        mesh=mesh,
        in_specs=(rows, rows, rows, rows, P(), P()),
        out_specs=(rows, rows, rows, rows),
        check_vma=False,
    )
```

```python
import functools
import math

import jax
import jax.numpy as jnp
from jax import lax
from jax.experimental import pallas as pl
from jax.experimental.pallas import tpu as pltpu
from jax.sharding import PartitionSpec as P

MESH = pl.DeviceIdType.MESH
NY, NZ, NH = 4, 8, 8
QB, BS, DH, RAND = 6, 128, 128, 3
ROWS = QB * BS
PART = ROWS // NH
LIST = 8 * BS
CHUNK = 256
NEAR, FAR = 5 * BS, RAND * BS
CHUNKS = NH * ROWS // CHUNK
PIECE = BS // NZ
SLOTS = QB * RAND
SCALE = 1.0 / math.sqrt(DH)
LOG2E = 1.4426950408889634
F32, BF16 = jnp.float32, jnp.bfloat16

T_WANT, T_PICK, T_OWN, T_SLOT, T_GLOB = 0, 32, 64, 82, 114


def dot(a, b, dims):
    return lax.dot_general(a, b, (dims, ((), ())), preferred_element_type=F32)


def flag(a, b):
    return (a == b).astype(jnp.int32).astype(F32)


def body(
    tab, q_in, g_in, kv_s, o_out, dq_out, dkv_out, o_end,
    qh, gh, r0, rp1, rp2, rp3, rm1, rm2, rm3, r4, xs, xr, edge,
    lkn, lvn, lktn, lvtn, lkf, lvf, lktf, lvtf, exn, dsf, o1, stats, ob, dqb,
    awk, awv, agk, agv, ark, arv,
    ys, yr, es, er, partp, partm, fin, ssp, ssm, srp, srm, dkvb,
    ga, gy, gp, gz, gm, gf, gall, raw,
    head_ss, head_rs, q_ss, q_rs, g_ss, g_rs, loc,
    zp_ss, zp_rs, zm_ss, zm_rs, e_ss, e_rs, y_ss, y_rs,
    a0_ss, a0_rs, a1_ss, a1_rs, a2_ss, a2_rs, a3_ss, a3_rs,
    o_ss, o_rs, dq_ss, dq_rs, w_ss, w_rs, e2_ss, e2_rs,
    pp_ss, pp_rs, pm_ss, pm_rs, dkv_ss, dkv_rs,
):
    blk = lax.axis_index("blk")
    head = lax.axis_index("head")
    y, z = blk // NZ, blk % NZ
    x, core = head // 2, head % 2
    up = (y * NZ + (z + 1) % NZ, head)
    down = (y * NZ + (z + NZ - 1) % NZ, head)
    after = ((blk + 1) % (NY * NZ), head)
    before = ((blk + NY * NZ - 1) % (NY * NZ), head)

    def column(dy):
        return (((y + dy) % NY) * NZ + z, head)

    def ring(dz):
        return (y * NZ + (z + dz) % NZ, head)

    def peer(k):
        t = k // 2
        return ((x + t * (t + 1) // 2) % (NH // 2)) * 2 + (core + k) % 2

    def remote(src, dst, ss, rs, dev):
        return pltpu.make_async_remote_copy(
            src_ref=src, dst_ref=dst, send_sem=ss, recv_sem=rs, device_id=dev, device_id_type=MESH
        )

    raw_q = pltpu.make_async_copy(q_in, raw, loc.at[6])
    raw_g = pltpu.make_async_copy(g_in, raw, loc.at[7])
    raw_q.start()
    bar = pltpu.get_barrier_semaphore()

    def greet(dev):
        pl.semaphore_signal(bar, inc=1, device_id=dev, device_id_type=MESH)

    def greet_head(k, c):
        greet((blk, (head + k) % NH))
        return c

    lax.fori_loop(1, NH, greet_head, 0)
    for dev in (after, before):
        greet(dev)
    for dy in range(1, NY):
        greet(column(dy))

    def greet_ring(dz, c):
        greet(ring(dz))
        return c

    lax.fori_loop(1, NZ, greet_ring, 0)
    pl.semaphore_wait(bar, NH - 1 + 2 + NY - 1 + NZ - 1)

    mine = pl.ds(pl.multiple_of(head * PART, 32), PART)
    rows_mine = pl.ds(pl.multiple_of(head * ROWS, 256), ROWS)

    def there_rows(h):
        return pl.ds(pl.multiple_of(h * ROWS, 256), ROWS)

    def kv_copy(h, half):
        return remote(
            kv_s.at[h, half], r0.at[half, mine, :], head_ss.at[half, h], head_rs.at[half, head], (blk, h)
        )

    def kv_arrival(h, half):
        there = pl.ds(pl.multiple_of(h * PART, 32), PART)
        return remote(
            kv_s.at[h, half], r0.at[half, there, :], head_ss.at[half, h], head_rs.at[half, h], (blk, h)
        )

    def q_copy(h):
        return remote(ob.at[there_rows(h), :], qh.at[rows_mine, :], q_ss.at[h], q_rs.at[head], (blk, h))

    def g_copy(h):
        return remote(dqb.at[there_rows(h), :], gh.at[rows_mine, :], g_ss.at[h], g_rs.at[head], (blk, h))

    def q_arrival(h):
        there = pl.ds(pl.multiple_of(h * ROWS, 256), ROWS)
        return remote(ob.at[there_rows(h), :], qh.at[there, :], q_ss.at[h], q_rs.at[h], (blk, h))

    def g_arrival(h):
        there = pl.ds(pl.multiple_of(h * ROWS, 256), ROWS)
        return remote(dqb.at[there_rows(h), :], gh.at[there, :], g_ss.at[h], g_rs.at[h], (blk, h))

    own_kv = pltpu.make_async_copy(kv_s.at[head], r0.at[:, mine, :], loc.at[0])
    own_q = pltpu.make_async_copy(ob.at[rows_mine, :], qh.at[rows_mine, :], loc.at[1])
    own_g = pltpu.make_async_copy(dqb.at[rows_mine, :], gh.at[rows_mine, :], loc.at[2])
    own_kv.start()

    def send_k(k, c):
        kv_copy(peer(k), 0).start()
        return c

    def send_v(k, c):
        kv_copy(peer(k), 1).start()
        return c

    def send_q(k, c):
        q_copy(peer(k)).start()
        return c

    def send_g(k, c):
        g_copy(peer(k)).start()
        return c

    lax.fori_loop(1, NH, send_k, 0)
    lax.fori_loop(1, NH, send_v, 0)

    def regroup(dst):
        for h in range(NH):
            rows = raw[:, h * NH:(h + 1) * NH, :].astype(F32).reshape(ROWS, DH)
            dst[h * ROWS:(h + 1) * ROWS, :] = rows.astype(BF16)

    raw_q.wait()
    regroup(ob)
    raw_g.start()
    zero = jnp.zeros((BS, DH), F32)
    for ref in (awk, awv, agk, agv, ark, arv):
        def clear(n, c, ref=ref):
            ref[pl.ds(pl.multiple_of(n * BS, BS), BS), :] = zero
            return c
        lax.fori_loop(0, ref.shape[0] // BS, clear, 0)

    own_kv.wait()

    def wait_kv(half):
        def one(k, c):
            kv_arrival((head + k) % NH, half).wait_recv()
            return c
        lax.fori_loop(1, NH, one, 0)

    plus = [r0, rp1, rp2, rp3, r4]
    minus = [r0, rm1, rm2, rm3, r4]

    def z_copy(step, half, upward):
        chain = plus if upward else minus
        ss, rs = (zp_ss, zp_rs) if upward else (zm_ss, zm_rs)
        return remote(
            chain[step].at[half], chain[step + 1].at[half],
            ss.at[step, half], rs.at[step, half], up if upward else down,
        )

    to_after = remote(r0.at[:, pl.ds(ROWS - BS, BS), :], edge.at[0], e_ss.at[0], e_rs.at[0], after)
    to_before = remote(r0.at[:, pl.ds(0, BS), :], edge.at[1], e_ss.at[1], e_rs.at[1], before)
    for half in (0, 1):
        wait_kv(half)
        z_copy(0, half, True).start()
        z_copy(0, half, False).start()
        if half == 0:
            own_q.start()
            lax.fori_loop(1, NH, send_q, 0)
    to_after.start()
    to_before.start()

    glob = [tab[T_GLOB + j] for j in range(2)]
    g_within = [tab[T_GLOB + 2 + j] for j in range(2)]

    def ar_y(n, dy):
        return remote(ga.at[n, (y + dy) % NY], gy.at[n, y], a0_ss.at[n, dy], a0_rs.at[n, NY - dy], column(dy))

    def ar_z(n, dz):
        rows = pl.ds(pl.multiple_of(((z + dz) % NZ) * PIECE, PIECE), PIECE)
        return remote(gp.at[n, rows, :], gz.at[n, z], a1_ss.at[n, dz], a1_rs.at[n, NZ - dz], ring(dz))

    z_rows = pl.ds(pl.multiple_of(z * PIECE, PIECE), PIECE)

    def ar_zback(n, dz):
        return remote(gm.at[n], gf.at[n, z_rows, :], a2_ss.at[n, dz], a2_rs.at[n, NZ - dz], ring(dz))

    def ar_yback(n, dy):
        return remote(gf.at[n], gall.at[n, y], a3_ss.at[n, dy], a3_rs.at[n, NY - dy], column(dy))

    def each(count, make, what):
        def one(d, c):
            copy = make(d)
            copy.start() if what == "start" else copy.wait_send()
            return c
        lax.fori_loop(1, count, one, 0)

    def ar_start(n):
        each(NY, functools.partial(ar_y, n), "start")
        gy[n, y] = ga[n, y]

    def ar_one(n):
        for dy in range(1, NY):
            remote(ga.at[n, y], gy.at[n, (y + dy) % NY], a0_ss.at[n, dy], a0_rs.at[n, dy], column(dy)).wait_recv()
        total = gy[n, 0].astype(F32)
        for k in range(1, NY):
            total += gy[n, k].astype(F32)
        gp[n] = total.astype(BF16)
        each(NZ, functools.partial(ar_z, n), "start")
        gz[n, z] = gp[n, z_rows, :]

    def ar_two(n):
        for dz in range(1, NZ):
            remote(gm.at[n], gz.at[n, (z + dz) % NZ], a1_ss.at[n, dz], a1_rs.at[n, dz], ring(dz)).wait_recv()
        total = gz[n, 0].astype(F32)
        for k in range(1, NZ):
            total += gz[n, k].astype(F32)
        gm[n] = total.astype(BF16)
        each(NZ, functools.partial(ar_zback, n), "start")
        gf[n, z_rows, :] = gm[n]

    def ar_three(n):
        for dz in range(1, NZ):
            rows = pl.ds(pl.multiple_of(((z + dz) % NZ) * PIECE, PIECE), PIECE)
            remote(gm.at[n], gf.at[n, rows, :], a2_ss.at[n, dz], a2_rs.at[n, dz], ring(dz)).wait_recv()
        each(NY, functools.partial(ar_yback, n), "start")
        gall[n, y] = gf[n]

    def ar_end(n):
        for dy in range(1, NY):
            remote(gf.at[n], gall.at[n, (y + dy) % NY], a3_ss.at[n, dy], a3_rs.at[n, dy], column(dy)).wait_recv()

    def ar_drain(n):
        each(NY, functools.partial(ar_y, n), "wait")
        each(NZ, functools.partial(ar_z, n), "wait")
        each(NZ, functools.partial(ar_zback, n), "wait")
        each(NY, functools.partial(ar_yback, n), "wait")

    def block_rows(w):
        return pl.ds(w * BS, BS)

    def y_copy(dy, index, shard_z):
        dev = column(dy)
        return remote(
            xs.at[index * 4 + dy], xr.at[y * NZ + shard_z],
            y_ss.at[index, dy], y_rs.at[index, (NY - dy) % NY], dev,
        )

    def y_arrival(dy, index, shard_z):
        return remote(
            xs.at[index * 4 + dy], xr.at[((y + dy) % NY) * NZ + shard_z],
            y_ss.at[index, dy], y_rs.at[index, dy], column(dy),
        )

    order = [(r0, 0), (rp1, -1), (rm1, 1), (rp2, -2), (rm2, 2), (rp3, -3), (rm3, 3), (r4, 4)]

    def shard_of(delta):
        return (z + delta + NZ) % NZ

    def serve(index):
        buf, delta = order[index]
        sz = shard_of(delta)

        def one(dy, c):
            w = tab[T_PICK + ((y + dy) % NY) * NZ + sz]
            xs[index * 4 + dy] = buf[:, block_rows(w), :]
            y_copy(dy, index, sz).start()
            return c

        lax.fori_loop(1, NY, one, 0)
        w = tab[T_PICK + y * NZ + sz]
        xr[y * NZ + sz] = buf[:, block_rows(w), :]
    def place(i, s, kb, vb):
        if s < 5:
            k_list, v_list, kt_list, vt_list, at = lkn, lvn, lktn, lvtn, s * BS
        else:
            k_list, v_list, kt_list, vt_list, at = lkf, lvf, lktf, lvtf, (s - 5) * BS
        k_list[i, at:at + BS, :] = kb
        v_list[i, at:at + BS, :] = vb
        kt_list[i, :, at:at + BS] = turned(kb)
        vt_list[i, :, at:at + BS] = turned(vb)

    def turned(block):
        return block.astype(F32).T.astype(BF16)

    def place_window(e, kb, vb):
        for s in range(3):
            if 0 <= e - s < QB:
                place(e - s, s, kb, vb)

    def chunks_of(h):
        js = [h * 3 + t for t in range(3)]
        return js, [j // 4 for j in js], [pl.ds(pl.multiple_of(j * CHUNK, CHUNK), CHUNK) for j in js]

    turns = range(3)
    nt, nn = ((1,), (1,)), ((1,), (0,))

    def attend_near(h):
        js, at, rows = chunks_of(h)
        st = [dot(lkn[at[t]], qh[rows[t], :], nt) for t in turns]
        peak = [jnp.max(v, axis=0, keepdims=True) for v in st]
        ex = [jnp.exp2((st[t] - peak[t]) * (SCALE * LOG2E)) for t in turns]
        total = [jnp.sum(v, axis=0, keepdims=True) for v in ex]
        eb = [v.astype(BF16) for v in ex]
        ot = [dot(lvtn[at[t]], eb[t], nn) for t in turns]
        for t in turns:
            exn[js[t]] = eb[t]
            o1[js[t]] = ot[t]
            stats[js[t], 0:1, :] = peak[t]
            stats[js[t], 1:2, :] = total[t]

    def attend_far(h):
        js, at, rows = chunks_of(h)
        q = [qh[r, :] for r in rows]
        g = [gh[r, :] for r in rows]
        first = [stats[j, 0:1, :] for j in js]
        first_total = [stats[j, 1:2, :] for j in js]
        first_out = [o1[j] for j in js]
        st = [dot(lkf[at[t]], q[t], nt) for t in turns]
        dpt = [dot(lvf[at[t]], g[t], nt) for t in turns]
        gt = [v.astype(F32).T for v in g]
        peak = [jnp.maximum(first[t], jnp.max(st[t], axis=0, keepdims=True)) for t in turns]
        shrink = [jnp.exp2((first[t] - peak[t]) * (SCALE * LOG2E)) for t in turns]
        ex = [jnp.exp2((st[t] - peak[t]) * (SCALE * LOG2E)) for t in turns]
        inv = [1.0 / (shrink[t] * first_total[t] + jnp.sum(ex[t], axis=0, keepdims=True)) for t in turns]
        near = [shrink[t] * inv[t] for t in turns]
        pt = [ex[t] * inv[t] for t in turns]
        pb = [v.astype(BF16) for v in pt]
        ot = [first_out[t] * near[t] + dot(lvtf[at[t]], pb[t], nn) for t in turns]
        delta = [jnp.sum(ot[t].astype(BF16).astype(F32) * gt[t], axis=0, keepdims=True) for t in turns]
        ds = [(pt[t] * (dpt[t] - delta[t])).astype(BF16) for t in turns]
        dv = [dot(pb[t], g[t], nn) for t in turns]
        dk = [dot(ds[t], q[t], nn) for t in turns]
        for t in turns:
            ob[rows[t], :] = ot[t].T.astype(BF16)
            stats[js[t], 2:3, :] = near[t]
            stats[js[t], 3:4, :] = delta[t]
            dsf[js[t]] = ds[t]
        for t in turns:
            rbase = pl.ds(pl.multiple_of(at[t] * FAR, BS), FAR)
            arv[rbase, :] += dv[t]
            ark[rbase, :] += dk[t]

    def attend_back(h):
        js, at, rows = chunks_of(h)
        q = [qh[r, :] for r in rows]
        g = [gh[r, :] for r in rows]
        dpt = [dot(lvn[at[t]], g[t], nt) for t in turns]
        pt = [exn[js[t]].astype(F32) * stats[js[t], 2:3, :] for t in turns]
        pb = [v.astype(BF16) for v in pt]
        ds = [(pt[t] * (dpt[t] - stats[js[t], 3:4, :])).astype(BF16) for t in turns]
        dqt = [dot(lktn[at[t]], ds[t], nn) + dot(lktf[at[t]], dsf[js[t]], nn) for t in turns]
        dv = [dot(pb[t], g[t], nn) for t in turns]
        dk = [dot(ds[t], q[t], nn) for t in turns]
        for t in turns:
            dqb[rows[t], :] = (dqt[t] * SCALE).T.astype(BF16)
        for t in turns:
            base = pl.ds(pl.multiple_of(at[t] * BS, BS), 3 * BS)
            awk[base, :] += dk[t][0:3 * BS]
            awv[base, :] += dv[t][0:3 * BS]
        agk[...] += dk[0][3 * BS:] + dk[1][3 * BS:] + dk[2][3 * BS:]
        agv[...] += dv[0][3 * BS:] + dv[1][3 * BS:] + dv[2][3 * BS:]

    def near_parts(first, last):
        def part(k, c):
            h = peer(k)

            @pl.when(k > 0)
            def _():
                q_arrival(h).wait_recv()

            attend_near(h)
            return c

        lax.fori_loop(first, last, part, 0)

    for j in range(2):
        here = flag(tab[T_GLOB + 4 + j], blk)
        for half in range(2):
            picked = r0[half, block_rows(g_within[j]), :].astype(F32)
            ga[0, 2 * j + half] = (picked * here).astype(BF16)
    ar_start(0)
    serve(0)
    raw_g.wait()
    regroup(dqb)
    for e in range(1, QB + 1):
        place_window(e, r0[0, (e - 1) * BS:e * BS, :], r0[1, (e - 1) * BS:e * BS, :])
    ar_one(0)

    def forward(step, half):
        z_copy(step - 1, half, True).wait_recv()
        if step < 3 or half == 0:
            z_copy(step, half, True).start()
        z_copy(step - 1, half, False).wait_recv()
        if step < 3 or half == 1:
            z_copy(step, half, False).start()

    forward(1, 0)
    to_after.wait_recv()
    to_before.wait_recv()
    place_window(0, edge[0, 0], edge[0, 1])
    place_window(QB + 1, edge[1, 0], edge[1, 1])
    ar_two(0)
    forward(1, 1)
    own_g.start()
    lax.fori_loop(1, NH, send_g, 0)
    serve(1)
    serve(2)
    forward(2, 0)
    ar_three(0)
    forward(2, 1)
    serve(3)
    serve(4)
    ar_end(0)
    for j in range(2):
        for i in range(QB):
            place(i, 3 + j, gall[0, 2 * j], gall[0, 2 * j + 1])
    own_q.wait()
    forward(3, 0)
    near_parts(0, 2)
    forward(3, 1)
    serve(5)
    serve(6)
    near_parts(2, 4)
    z_copy(3, 0, True).wait_recv()
    z_copy(3, 1, False).wait_recv()
    serve(7)
    near_parts(4, 8)

    for index in range(8):
        def wait_y(dy, c, index=index):
            y_arrival(dy, index, shard_of(order[index][1])).wait_recv()
            return c
        lax.fori_loop(1, NY, wait_y, 0)

    def place_random(i, c):
        for r in range(RAND):
            owner = tab[T_OWN + i * RAND + r]
            place(i, 5 + r, xr[owner, 0], xr[owner, 1])
        return c

    lax.fori_loop(0, QB, place_random, 0)
    own_g.wait()

    def wait_g(k, c):
        g_arrival(peer(k)).wait_recv()
        return c

    lax.fori_loop(1, NH, wait_g, 0)

    def o_copy(h):
        return remote(ob.at[there_rows(h), :], o_out.at[rows_mine, :], o_ss.at[h], o_rs.at[head], (blk, h))

    def dq_copy(h):
        return remote(dqb.at[there_rows(h), :], dq_out.at[rows_mine, :], dq_ss.at[h], dq_rs.at[head], (blk, h))

    def o_arrival(h):
        return remote(ob.at[there_rows(h), :], o_out.at[there_rows(h), :], o_ss.at[h], o_rs.at[h], (blk, h))

    def dq_arrival(h):
        return remote(dqb.at[there_rows(h), :], dq_out.at[there_rows(h), :], dq_ss.at[h], dq_rs.at[h], (blk, h))

    own_o = pltpu.make_async_copy(ob.at[there_rows(head), :], o_out.at[rows_mine, :], loc.at[3])
    own_dq = pltpu.make_async_copy(dqb.at[there_rows(head), :], dq_out.at[rows_mine, :], loc.at[4])

    def far_part(n, c):
        k = NH - 1 - n
        h = peer(k)
        attend_far(h)

        @pl.when(k > 0)
        def _():
            o_copy(h).start()

        return c

    def staging_free(k, c):
        h = peer(k)
        q_copy(h).wait_send()
        g_copy(h).wait_send()
        return c

    lax.fori_loop(1, NH, staging_free, 0)
    lax.fori_loop(0, NH, far_part, 0)
    own_o.start()

    def back_parts(first, last):
        def part(n, c):
            k = NH - 1 - n
            h = peer(k)
            attend_back(h)

            @pl.when(k > 0)
            def _():
                dq_copy(h).start()

            return c

        lax.fori_loop(first, last, part, 0)

    def w_copy(dy, index):
        return remote(
            ys.at[index * 4 + dy], yr.at[index * 4 + y],
            w_ss.at[index, dy], w_rs.at[index, (NY - dy) % NY], column(dy),
        )

    def w_arrival(dy, index):
        return remote(
            ys.at[index * 4 + dy], yr.at[index * 4 + (y + dy) % NY],
            w_ss.at[index, dy], w_rs.at[index, dy], column(dy),
        )

    back = [4, 3, -3, 2, -2, 1, -1, 0]

    def slot_rows(slot):
        return pl.ds(slot * BS, BS)

    def gather_in(arrival, own, out, dst, n):
        own.wait()

        def one(k, c):
            arrival(peer(k)).wait_recv()
            return c

        lax.fori_loop(1, NH, one, 0)
        pltpu.make_async_copy(out, dst, loc.at[n]).start()

    def gather_out(out, dst, end, n):
        pltpu.make_async_copy(out, dst, loc.at[n]).wait()
        for pair in range(NH // 2):
            two = [
                dst[h * ROWS:(h + 1) * ROWS, :].astype(F32).reshape(PART, NH, DH) for h in (2 * pair, 2 * pair + 1)
            ]
            raw[:, pair * 2 * NH:(pair + 1) * 2 * NH, :] = jnp.concatenate(two, axis=1).astype(BF16)
        pltpu.make_async_copy(raw, end, loc.at[n + 1]).start()

    def give(index):
        sz = shard_of(back[index])

        def one(dy, c):
            slot = tab[T_SLOT + ((y + dy) % NY) * NZ + sz]
            ys[index * 4 + dy, 0] = (ark[slot_rows(slot), :] * SCALE).astype(BF16)
            ys[index * 4 + dy, 1] = arv[slot_rows(slot), :].astype(BF16)
            w_copy(dy, index).start()
            return c

        lax.fori_loop(1, NY, one, 0)
        slot = tab[T_SLOT + y * NZ + sz]
        yr[index * 4 + y, 0] = (ark[slot_rows(slot), :] * SCALE).astype(BF16)
        yr[index * 4 + y, 1] = arv[slot_rows(slot), :].astype(BF16)

    def add_up(index, part):
        sz = shard_of(back[index])

        def wait_w(dy, c):
            w_arrival(dy, index).wait_recv()
            return c

        lax.fori_loop(1, NY, wait_w, 0)
        hits = [tab[T_WANT + yy * NZ + sz] for yy in range(NY)]

        def one_block(b, c):
            for half in range(2):
                total = yr[index * 4, half].astype(part.dtype) * flag(hits[0], b).astype(part.dtype)
                for yy in range(1, NY):
                    total += yr[index * 4 + yy, half].astype(part.dtype) * flag(hits[yy], b).astype(part.dtype)
                part[half, pl.ds(pl.multiple_of(b * BS, BS), BS), :] = total
            return c

        lax.fori_loop(0, QB, one_block, 0)

    def p_copy(step, half, upward):
        if upward:
            return remote(ssp.at[step, half], srp.at[step, half], pp_ss.at[step, half], pp_rs.at[step, half], up)
        return remote(ssm.at[step, half], srm.at[step, half], pm_ss.at[step, half], pm_rs.at[step, half], down)

    def pass_on(step):
        for half in (0, 1):
            for upward in (half == 1, half == 0):
                send, recv, part = (ssp, srp, partp) if upward else (ssm, srm, partm)
                total = part[half].astype(F32)
                if step > 1 or half == (0 if upward else 1):
                    p_copy(step - 1, half, upward).wait_recv()
                    total += recv[step - 1, half].astype(F32)
                send[step, half] = total.astype(BF16)
                p_copy(step, half, upward).start()

    give(0)
    give(1)
    give(2)
    back_parts(0, 4)
    add_up(0, partp)
    ssp[0, 0] = partp[0].astype(BF16)
    p_copy(0, 0, True).start()
    ssm[0, 1] = partp[1].astype(BF16)
    p_copy(0, 1, False).start()
    give(3)
    give(4)
    add_up(1, partp)
    add_up(2, partm)
    back_parts(4, 8)
    own_dq.start()
    for n, at in ((0, 0), (1, QB + 1)):
        rows = slice(at * BS, (at + 1) * BS)
        es[n, 0] = (awk[rows, :] * SCALE).astype(BF16)
        es[n, 1] = awv[rows, :].astype(BF16)
    e2_before = remote(es.at[0], er.at[1], e2_ss.at[0], e2_rs.at[1], before)
    e2_after = remote(es.at[1], er.at[0], e2_ss.at[1], e2_rs.at[0], after)
    e2_before.start()
    e2_after.start()
    for j in range(2):
        rows = slice(j * BS, (j + 1) * BS)
        ga[1, 2 * j] = (agk[rows, :] * SCALE).astype(BF16)
        ga[1, 2 * j + 1] = agv[rows, :].astype(BF16)
    ar_start(1)
    pass_on(1)
    give(5)
    give(6)
    ar_one(1)
    add_up(3, partp)
    add_up(4, partm)
    pass_on(2)
    give(7)
    ar_two(1)
    add_up(5, partp)
    add_up(6, partm)
    pass_on(3)
    gather_in(o_arrival, own_o, o_out, qh, 8)
    ar_three(1)
    gather_out(o_out, qh, o_end, 8)
    add_up(7, fin)
    e2_before.wait_send()
    e2_after.wait_send()
    remote(es.at[0], er.at[1], e2_ss.at[0], e2_rs.at[1], before).wait_recv()
    remote(es.at[1], er.at[0], e2_ss.at[1], e2_rs.at[0], after).wait_recv()
    for half, window in ((0, awk), (1, awv)):
        factor = SCALE if half == 0 else 1.0
        for b in range(QB):
            rows = slice(b * BS, (b + 1) * BS)
            total = window[(b + 1) * BS:(b + 2) * BS, :] * factor + fin[half, rows, :]
            if b == 0:
                total += er[0, half].astype(F32)
            if b == QB - 1:
                total += er[1, half].astype(F32)
            fin[half, rows, :] = total
    def part_rows(h):
        return pl.ds(pl.multiple_of(h * PART, 32), PART)

    def dkv_copy(h, half):
        return remote(
            dkvb.at[half, part_rows(h), :], dkv_out.at[head, half],
            dkv_ss.at[half, h], dkv_rs.at[half, head], (blk, h),
        )

    def dkv_arrival(h, half):
        return remote(
            dkvb.at[half, part_rows(h), :], dkv_out.at[h, half],
            dkv_ss.at[half, h], dkv_rs.at[half, h], (blk, h),
        )

    def own_dkv(half):
        return pltpu.make_async_copy(dkvb.at[half, mine, :], dkv_out.at[head, half], loc.at[0 if half else 5])

    def send_dkv(half, k, c):
        dkv_copy(peer(k), half).start()
        return c

    ar_end(1)
    for half in range(2):
        p_copy(3, half, True).wait_recv()
        p_copy(3, half, False).wait_recv()
        for b in range(QB):
            rows = slice(b * BS, (b + 1) * BS)
            total = fin[half, rows, :]
            total += srp[3, half, rows, :].astype(F32) + srm[3, half, rows, :].astype(F32)
            for j in range(2):
                total += gall[1, 2 * j + half].astype(F32) * flag(glob[j], blk * QB + b)
            dkvb[half, rows, :] = total.astype(BF16)
        own_dkv(half).start()
        lax.fori_loop(1, NH, functools.partial(send_dkv, half), 0)

    pltpu.make_async_copy(raw, o_end, loc.at[9]).wait()

    def drain(k, c):
        h = (head + k) % NH
        kv_copy(h, 0).wait_send()
        kv_copy(h, 1).wait_send()
        o_copy(h).wait_send()
        dq_copy(h).wait_send()
        dkv_copy(h, 0).wait_send()
        dkv_copy(h, 1).wait_send()
        dq_arrival(h).wait_recv()
        dkv_arrival(h, 0).wait_recv()
        dkv_arrival(h, 1).wait_recv()
        return c

    for step in range(4):
        for half in range(2):
            if step < 3 or half == 0:
                z_copy(step, half, True).wait_send()
            if step < 3 or half == 1:
                z_copy(step, half, False).wait_send()
            if step > 0 or half == 0:
                p_copy(step, half, True).wait_send()
            if step > 0 or half == 1:
                p_copy(step, half, False).wait_send()
    to_after.wait_send()
    to_before.wait_send()

    def drain_column(dy, c):
        for index in range(8):
            y_copy(dy, index, shard_of(order[index][1])).wait_send()
            w_copy(dy, index).wait_send()
        return c

    lax.fori_loop(1, NY, drain_column, 0)
    ar_drain(0)
    ar_drain(1)
    lax.fori_loop(1, NH, drain, 0)
    own_dq.wait()
    own_dkv(0).wait()
    own_dkv(1).wait()


def tables(rand_blocks, global_blocks):
    blk = lax.axis_index("blk")
    head = lax.axis_index("head")
    y, z = blk // NZ, blk % NZ
    chosen = lax.dynamic_slice_in_dim(rand_blocks, head, 1, 1).reshape(NY, NZ, SLOTS)
    column = lax.dynamic_slice_in_dim(chosen, z, 1, 1)
    owners = y * NZ + jnp.arange(NZ, dtype=jnp.int32)[None, :, None]
    want = jnp.max(jnp.where(column // QB == owners, column % QB, -1), axis=2)
    own = lax.dynamic_slice_in_dim(chosen.reshape(NY * NZ, SLOTS), blk, 1, 0)[0] // QB
    shards = jnp.arange(NY * NZ, dtype=jnp.int32)[:, None]
    slot = jnp.max(
        jnp.where(own[None, :] == shards, jnp.arange(SLOTS, dtype=jnp.int32)[None, :], 0), axis=1
    )
    want = want.reshape(-1)
    picked = jnp.maximum(want, 0)
    shard = global_blocks // QB
    return jnp.concatenate(
        [want, picked, own, slot, global_blocks, global_blocks % QB, shard]
    )


def on_device(queries, keys, values, out_grad, rand_blocks, global_blocks):
    tab = tables(rand_blocks, global_blocks)
    kv_s = jnp.stack([keys, values]).transpose(2, 0, 1, 3)
    vm = lambda shape, dtype=BF16: pltpu.VMEM(shape, dtype)
    dma = lambda *shape: pltpu.SemaphoreType.DMA(shape)
    total = NH * ROWS
    pair = (2, BS, DH)
    anywhere = pl.BlockSpec(memory_space=pl.ANY)
    _, dq_h, dkv_h, attn_out = pl.pallas_call(
        body,
        out_shape=(
            jax.ShapeDtypeStruct((total, DH), BF16),
            jax.ShapeDtypeStruct((total, DH), BF16),
            jax.ShapeDtypeStruct((NH, 2, PART, DH), BF16),
            jax.ShapeDtypeStruct(queries.shape, BF16),
        ),
        in_specs=[pl.BlockSpec(memory_space=pltpu.SMEM), anywhere, anywhere, anywhere],
        out_specs=(anywhere,) * 4,
        scratch_shapes=[
            vm((total, DH)), vm((total, DH)),
            *[vm((2, ROWS, DH)) for _ in range(8)],
            vm((32,) + pair), vm((32,) + pair), vm((2,) + pair),
            vm((QB, NEAR, DH)), vm((QB, NEAR, DH)), vm((QB, DH, NEAR)), vm((QB, DH, NEAR)),
            vm((QB, FAR, DH)), vm((QB, FAR, DH)), vm((QB, DH, FAR)), vm((QB, DH, FAR)),
            vm((CHUNKS, NEAR, CHUNK)), vm((CHUNKS, FAR, CHUNK)), vm((CHUNKS, DH, CHUNK), F32),
            vm((CHUNKS, 8, CHUNK), F32),
            vm((total, DH)), vm((total, DH)),
            vm(((QB + 2) * BS, DH), F32), vm(((QB + 2) * BS, DH), F32),
            vm((2 * BS, DH), F32), vm((2 * BS, DH), F32),
            vm((SLOTS * BS, DH), F32), vm((SLOTS * BS, DH), F32),
            vm((32,) + pair), vm((32,) + pair), vm((2,) + pair), vm((2,) + pair),
            vm((2, ROWS, DH)), vm((2, ROWS, DH)), vm((2, ROWS, DH), F32),
            *[vm((4, 2, ROWS, DH)) for _ in range(4)],
            vm((2, ROWS, DH)),
            vm((2, NY, BS, DH)), vm((2, NY, BS, DH)), vm((2, BS, DH)), vm((2, NZ, PIECE, DH)),
            vm((2, PIECE, DH)), vm((2, BS, DH)), vm((2, NY, BS, DH)),
            vm(queries.shape),
            dma(2, NH), dma(2, NH), dma(NH), dma(NH), dma(NH), dma(NH), dma(10),
            dma(4, 2), dma(4, 2), dma(4, 2), dma(4, 2), dma(2), dma(2), dma(8, NY), dma(8, NY),
            dma(2, NY), dma(2, NY), dma(2, NZ), dma(2, NZ), dma(2, NZ), dma(2, NZ), dma(2, NY), dma(2, NY),
            dma(NH), dma(NH), dma(NH), dma(NH), dma(8, NY), dma(8, NY), dma(2), dma(2),
            dma(4, 2), dma(4, 2), dma(4, 2), dma(4, 2), dma(2, NH), dma(2, NH),
        ],
        compiler_params=pltpu.CompilerParams(
            collective_id=0, has_side_effects=True, vmem_limit_bytes=62 * 2**20
        ),
    )(tab, queries, out_grad, kv_s)

    query_grad = dq_h.reshape(NH, PART, -1, DH).transpose(1, 0, 2, 3).reshape(queries.shape)
    kv_back = dkv_h.transpose(1, 2, 0, 3)
    return attn_out, query_grad, kv_back[0], kv_back[1]


def solution(mesh):
    rows = P(("blk", "head"), None, None)
    return jax.shard_map(
        on_device,
        mesh=mesh,
        in_specs=(rows, rows, rows, rows, P(), P()),
        out_specs=(rows, rows, rows, rows),
        check_vma=False,
    )
```
